512 devices in a mesh: dp: 8 (over x, core), expert: 64 (over z, y).
Axes of the slice: x: 4, y: 8, z: 8, core: 2. Of those that a mesh axis runs over, the one named last changes fastest.
Arguments:
- tokens: bfloat16 [65536, 2048], P(('dp', 'expert')), may hold values from -6 to 6
- routes: int32 [65536, 2], P(('dp', 'expert')), may hold values from 0 to 63, all different within a row; in each aligned block of 128 rows (0 to 127, 128 to 255, ...) at most 6 rows name the same one
- route_gates: bfloat16 [65536, 2], P(('dp', 'expert')), may hold values from 0.049804688 to 0.5
- out_grad: bfloat16 [65536, 2048], P(('dp', 'expert')), may hold values from -3 to 3
- w_gate: bfloat16 [64, 2048, 384], P('expert', 'dp'), may hold values from -0.125 to 0.125
- w_up: bfloat16 [64, 2048, 384], P('expert', 'dp'), may hold values from -0.125 to 0.125
- w_down: bfloat16 [64, 384, 2048], P('expert', 'dp'), may hold values from -0.3125 to 0.3125
Outputs:
- token_grad: bfloat16 [65536, 2048], P(('dp', 'expert'))
- gate_grad: bfloat16 [65536, 2], P(('dp', 'expert'))
- down_grad: bfloat16 [64, 384, 2048], P('expert', 'dp')
The draws below stay inside these ranges and needn't reach their ends.
Inputs may be any that keep to these rules, and one draw needn't show every extreme that they name: `routes`: each row names 2 different experts. Within each aligned block of 128 rows (the tokens of one device) no expert is named more than 6 times, and in some block some expert is named exactly 6 times.
All inputs are finite; a program needn't handle non-finite values.
Results may differ from the reference program's by a relative error of at most 0.019.
Values may be sent and summed in bfloat16 or wider, within the bound.
No kernel may reach another device: no remote copies, remote signals or barrier semaphores. Data moves between devices by JAX's collectives and lax.ppermute only.
A program may use at most 64 MiB of HBM per device.

```python
import math
import jax
import jax.numpy as jnp
import numpy as np
from jax import lax

D = 2048
HID = 384
TOP = 2
TOK_DEV = 128
EXPERTS = 64
CAP = 6
TOKENS = 65536


def block_scale(rng, shape, pieces, low, high):
    gain, own = 1.0, jax.random.fold_in(rng, 6)
    for axis_at, parts in pieces:
        steps = jnp.exp(jax.random.uniform(jax.random.fold_in(own, axis_at), (parts,), jnp.float32, low / len(pieces), high / len(pieces)))
        gain = gain * jnp.repeat(steps, shape[axis_at] // parts).reshape([-1 if axis == axis_at else 1 for axis in range(len(shape))])
    return gain


def deal_out(key, own, number, rows, count, top, limit, slope):
    order = jax.random.permutation(key, count)
    crowded, ordinary = load_shares(count, rows * top, limit, slope, True), load_shares(count, rows * top, limit, slope, False)
    places = jnp.arange(count)

    def named(tallies, turn):
        used = int((tallies > 0).sum())
        fixed = max(1, used // 4)
        moved = fixed + (places - fixed + turn * (used - fixed)) % max(1, count - fixed)
        return jnp.zeros((count,), jnp.int32).at[order[jnp.where(places < fixed, places, moved)]].set(jnp.asarray(tallies, jnp.int32))

    tallies = jnp.where(number % 4 == 0, named(crowded, number // 4), named(ordinary, number - number // 4 - 1))
    mixed = jax.random.permutation(jax.random.fold_in(own, 3), count)
    donor, sink = mixed[0:count // 2 * 2:2], mixed[1:count // 2 * 2:2]
    slack = jnp.minimum(tallies[donor] - 1, limit - tallies[sink]) // 2
    slack = jnp.where((donor == order[0]) | (sink == order[0]) | (tallies[sink] == 0), 0, jnp.maximum(slack, 0))
    moved = jax.random.randint(jax.random.fold_in(own, 4), (count // 2,), 0, 1 << 20) % (slack + 1)
    tallies = tallies.at[donor].add(-moved).at[sink].add(moved)
    items = jnp.searchsorted(jnp.cumsum(tallies), jnp.arange(rows * top), side="right").astype(jnp.int32)
    grid = items.reshape(top, rows).T
    grid = grid[jax.random.permutation(jax.random.fold_in(own, 1), rows)]
    turn = jax.random.randint(jax.random.fold_in(own, 2), (rows, 1), 0, top)
    return jnp.take_along_axis(grid, (jnp.arange(top)[None, :] + turn) % top, axis=1)


def load_shares(number_of, total, most, slope, full):
    loads = [(1 << 20) // math.isqrt(grade ** slope) + 1 for grade in range(1, number_of + 1)]
    largest = most if full else min(most, max(-(-total // number_of), total * loads[0] // sum(loads)))
    least = 1 if total - largest >= number_of - 1 else 0
    given, surplus = [largest] + [least] * (number_of - 1), total - largest - least * (number_of - 1)
    while surplus > 0:
        movable = [i for i in range(1, number_of) if given[i] < largest] or [i for i in range(1, number_of) if given[i] < most]
        mass, budget = sum([loads[i] for i in movable]), surplus
        for i in movable:
            extra = min(most - given[i], max(1, budget * loads[i] // mass), surplus)
            given[i] = given[i] + extra
            surplus = surplus - extra
    return np.array(given)


def noise(rng, shape, width, most, shards=(), kind=jnp.bfloat16):
    loudness = block_scale(rng, shape, shards, -0.22, 0.18) if shards else 1.0
    array = jax.random.normal(rng, shape, jnp.float32) * width * loudness
    return jnp.minimum(jnp.maximum(array, -most), most).astype(kind)


def setup_inputs(seed: int = 0) -> dict:
    seeds = jax.random.split(jax.random.key(seed), 8)
    tokens = noise(seeds[0], (TOKENS, D), 1.0, 6.0, ((0, 512),))
    routes_keys = jax.random.split(jax.random.fold_in(seeds[1], 1), TOKENS // TOK_DEV)
    routes_turns = jax.random.permutation(jax.random.fold_in(seeds[1], 3), TOKENS // TOK_DEV)
    routes = jax.vmap(lambda own, number: deal_out(jax.random.fold_in(seeds[1], 2), own, number, TOK_DEV, EXPERTS, TOP, CAP, 2))(routes_keys, routes_turns).reshape((TOKENS, TOP))
    route_gates = jnp.clip(jnp.exp(math.log(0.5) - 2.306499 * jax.random.uniform(seeds[2], (TOKENS, TOP), jnp.float32) ** block_scale(seeds[2], (TOKENS, TOP), ((0, 512),), -0.2, 0.2)), 0.049804688, 0.5).astype(jnp.bfloat16)
    out_grad = noise(seeds[3], (TOKENS, D), 0.5, 3.0, ((0, 512),))
    w_gate = noise(seeds[4], (EXPERTS, D, HID), D ** -0.5, 0.125, ((0, 64), (1, 8)))
    w_up = noise(seeds[5], (EXPERTS, D, HID), D ** -0.5, 0.125, ((0, 64), (1, 8)))
    w_down = noise(seeds[6], (EXPERTS, HID, D), HID ** -0.5, 0.3125, ((0, 64), (1, 8)))
    return dict(tokens=tokens, routes=routes, route_gates=route_gates, out_grad=out_grad, w_gate=w_gate, w_up=w_up, w_down=w_down)


CONTRACT_LAST = (((1,), (1,)), ((), ()))
CONTRACT_FIRST = (((0,), (0,)), ((), ()))


def expert_pass(slot_inputs, slot_grads, slot_gates, gate_mat, up_mat, down_mat):
    pre_gate = jnp.dot(slot_inputs, gate_mat, preferred_element_type=jnp.float32)
    pre_up = jnp.dot(slot_inputs, up_mat, preferred_element_type=jnp.float32)
    squash = jax.nn.sigmoid(pre_gate)
    activated = pre_gate * squash
    hidden = (activated * pre_up).astype(jnp.bfloat16)
    outputs = jnp.dot(hidden, down_mat, preferred_element_type=jnp.float32).astype(jnp.bfloat16)
    scaled = (slot_gates[:, None] * slot_grads.astype(jnp.float32)).astype(jnp.bfloat16)
    hidden_grad = lax.dot_general(scaled, down_mat, CONTRACT_LAST, preferred_element_type=jnp.float32)
    grad_gate = (hidden_grad * pre_up * squash * (1.0 + pre_gate * (1.0 - squash))).astype(jnp.bfloat16)
    grad_upper = (hidden_grad * activated).astype(jnp.bfloat16)
    input_grad = lax.dot_general(grad_gate, gate_mat, CONTRACT_LAST, preferred_element_type=jnp.float32)
    input_grad = input_grad + lax.dot_general(grad_upper, up_mat, CONTRACT_LAST, preferred_element_type=jnp.float32)
    down_term = lax.dot_general(hidden, scaled, CONTRACT_FIRST, preferred_element_type=jnp.float32)
    return outputs, input_grad.astype(jnp.bfloat16), down_term


def reference(tokens, routes, route_gates, out_grad, w_gate, w_up, w_down):
    block_count = TOKENS // TOK_DEV
    per_block = TOK_DEV * TOP
    pair_total = TOKENS * TOP
    slot_total = block_count * CAP
    flat_ids = routes.reshape(-1).astype(jnp.int32)

    def block_ranks(block_ids):
        matches = (block_ids[:, None] == jnp.arange(EXPERTS, dtype=jnp.int32)[None, :]).astype(jnp.int32)
        before = jnp.cumsum(matches, axis=0) - matches
        return jnp.sum(before * matches, axis=1).astype(jnp.int32)

    ranking = lax.map(block_ranks, flat_ids.reshape(block_count, per_block)).reshape(-1).astype(jnp.int32)
    pair_index = jnp.arange(pair_total, dtype=jnp.int32)
    owners = (pair_index // per_block).astype(jnp.int32)
    slot_of = (owners * CAP + ranking).astype(jnp.int32)
    token_of = (pair_index // TOP).astype(jnp.int32)
    gate_flat = route_gates.reshape(-1)

    def one_expert(totals, expert_id):
        grad_total, dot_total = totals
        target = jnp.where(flat_ids == expert_id, slot_of, slot_total).astype(jnp.int32)
        slot_token = jnp.zeros((slot_total + 1,), jnp.int32).at[target].set(token_of)[:slot_total]
        slot_pair = jnp.full((slot_total + 1,), pair_total, jnp.int32).at[target].set(pair_index)[:slot_total]
        live = slot_pair < pair_total
        slot_inputs = jnp.where(live[:, None], tokens[slot_token], jnp.zeros_like(tokens[slot_token]))
        slot_grads = jnp.where(live[:, None], out_grad[slot_token], jnp.zeros_like(out_grad[slot_token]))
        safe_pair = jnp.minimum(slot_pair, pair_total - 1).astype(jnp.int32)
        slot_gates = jnp.where(live, gate_flat[safe_pair].astype(jnp.float32), jnp.float32(0.0))
        outputs, input_grad, down_term = expert_pass(slot_inputs, slot_grads, slot_gates,
                                                     w_gate[expert_id], w_up[expert_id], w_down[expert_id])
        grad_total = grad_total.at[slot_token].add(
            jnp.where(live[:, None], input_grad.astype(jnp.float32), jnp.float32(0.0)))
        dots = jnp.einsum("sd,sd->s", slot_grads.astype(jnp.float32), outputs.astype(jnp.float32))
        dot_total = dot_total.at[slot_pair].set(dots)
        return (grad_total, dot_total), down_term.astype(jnp.bfloat16)

    start = (jnp.zeros((TOKENS, D), jnp.float32), jnp.zeros((pair_total + 1,), jnp.float32))
    (grad_total, dot_total), downs = lax.scan(one_expert, start, jnp.arange(EXPERTS, dtype=jnp.int32))
    token_grad = grad_total.astype(jnp.bfloat16)
    gate_grad = dot_total[:pair_total].reshape(TOKENS, TOP).astype(jnp.bfloat16)
    return token_grad, gate_grad, downs
```

```python
import functools

import jax
import jax.numpy as jnp
from jax import lax
from jax.experimental import pallas as pl
from jax.experimental.pallas import tpu as pltpu
from jax.sharding import PartitionSpec as P

BF = jnp.bfloat16
F32 = jnp.float32
NT = (((1,), (1,)), ((), ()))
TN = (((0,), (0,)), ((), ()))


def iota(shape, axis):
    return lax.broadcasted_iota(jnp.int32, shape, axis)


def slot_keys(routes_ref, experts):
    toks = routes_ref.shape[1]
    rows = iota((experts, toks), 0)
    first = routes_ref[0:1, :] == rows
    second = routes_ref[1:2, :] == rows
    named = jnp.where(first, 1.0, jnp.where(second, 1.0, 0.0))
    earlier = jnp.where(iota((toks, toks), 0) < iota((toks, toks), 1), 1.0, 0.0).astype(BF)
    before = jnp.dot(named.astype(BF), earlier, preferred_element_type=F32)
    return jnp.where(named > 0.5, before, -1.0), first, second


def dispatch_kernel(experts, cap, routes_ref, gates_ref, tokens_ref, grads_ref, send_ref, stacked_ref, out_ref, in_sems, out_sems):
    toks, dim = tokens_ref.shape
    half = dim // 2
    rows = 4 * cap
    loads = []
    for a, ref in enumerate((tokens_ref, grads_ref)):
        for c in range(2):
            at = 2 * a + c
            loads.append(pltpu.make_async_copy(
                ref.at[:, pl.ds(c * half, half)], stacked_ref.at[pl.ds(at * toks, toks), :], in_sems.at[at]
            ))
            loads[-1].start()
    keys, first, second = slot_keys(routes_ref, experts)
    gates = gates_ref[...].astype(F32)
    gate = jnp.where(first, gates[0:1, :], jnp.where(second, gates[1:2, :], 0.0))
    block = 16
    size = block * rows
    q = iota((block, rows, toks), 1)
    slot = (q % cap).astype(F32)
    kind = (q // cap) % 2
    part = q // (2 * cap)
    for load in loads:
        load.wait()
    stores = []
    for b in range(experts // block):
        key = keys[b * block:(b + 1) * block][:, None, :]
        g = gate[b * block:(b + 1) * block][:, None, :]
        value = jnp.where(key == slot, jnp.where(kind == 1, g, 1.0), 0.0)
        pieces = []
        for a in range(2):
            for c in range(2):
                piece = jnp.where((kind == a) & (part == c), value, 0.0)
                pieces.append(piece.reshape(size, toks).astype(BF))
        placing = jnp.concatenate(pieces, axis=1)
        out_ref[b * size:(b + 1) * size, :] = jnp.dot(
            placing, stacked_ref[...], preferred_element_type=F32
        ).astype(BF)
        at = pl.ds(b * size, size)
        stores.append(pltpu.make_async_copy(out_ref.at[at, :], send_ref.at[at, :], out_sems.at[b]))
        stores[-1].start()
    for store in stores:
        store.wait()


def expert_kernel(
    cap, recv_hbm, wgu_hbm, wd_hbm, ret_hbm, hidden_ref, scaled_ref, dots_ref,
    recv_ref, wgu_ref, wd_ref, x_ref, ggu_ref, part_ref, ret_ref, in_sems, recv_sems, out_sems,
):
    total, half = recv_ref.shape
    wide = ret_ref.shape[1]
    rows = 4 * cap
    block = 16
    size = block * rows
    count = block * cap
    blocks = total // size
    hid = wd_ref.shape[0]
    loads = []
    for b in range(blocks):
        at = pl.ds(b * size, size)
        loads.append(pltpu.make_async_copy(recv_hbm.at[at, :], recv_ref.at[at, :], recv_sems.at[b]))
        loads[-1].start()
    load_down = pltpu.make_async_copy(wd_hbm, wd_ref, in_sems.at[0])
    load_wgu = pltpu.make_async_copy(wgu_hbm, wgu_ref, in_sems.at[1])
    load_down.start()
    load_wgu.start()
    out_row = iota((size, 1), 0)
    in_row = iota((size, size), 1)
    group, inner = out_row // count, out_row % count
    wanted = (inner // cap) * rows + (group % 2) * (2 * cap) + (group // 2) * cap + inner % cap
    perm = jnp.where(wanted == in_row, 1.0, 0.0).astype(BF)
    for b in range(blocks):
        loads[b].wait()
        moved = jnp.dot(perm, recv_ref[b * size:(b + 1) * size, :], preferred_element_type=F32).astype(BF)
        at = slice(b * count, (b + 1) * count)
        x_ref[at, :half] = moved[0:count]
        x_ref[at, half:] = moved[count:2 * count]
        scaled_ref[at, :half] = moved[2 * count:3 * count]
        scaled_ref[at, half:] = moved[3 * count:]
    load_down.wait()
    hidden_grad = lax.dot_general(scaled_ref[...], wd_ref[...], NT, preferred_element_type=F32)
    load_wgu.wait()
    pre_gate = jnp.dot(x_ref[...], wgu_ref[:, :hid], preferred_element_type=F32)
    pre_up = jnp.dot(x_ref[...], wgu_ref[:, hid:], preferred_element_type=F32)
    squash = jax.nn.sigmoid(pre_gate)
    activated = pre_gate * squash
    hidden = (activated * pre_up).astype(BF)
    hidden_ref[...] = hidden
    ggu_ref[:, :hid] = (hidden_grad * pre_up * squash * (1.0 + pre_gate * (1.0 - squash))).astype(BF)
    ggu_ref[:, hid:] = (hidden_grad * activated).astype(BF)
    product = hidden.astype(F32) * hidden_grad
    folded = product[:, 0:128]
    for j in range(1, hid // 128):
        folded = folded + product[:, j * 128:(j + 1) * 128]
    dots_ref[...] = jnp.sum(folded.T, axis=0, keepdims=True)
    source, inner = out_row // rows, out_row % rows
    wanted = (inner // cap) * count + source * cap + inner % cap
    perm = jnp.where(wanted == in_row, 1.0, 0.0).astype(BF)
    for c in range(4):
        piece = lax.dot_general(
            ggu_ref[...], wgu_ref[c * wide:(c + 1) * wide, :], NT, preferred_element_type=F32
        ).astype(BF)
        for b in range(blocks):
            part_ref[b * size + c * count:b * size + (c + 1) * count, :] = piece[b * count:(b + 1) * count]
    stores = []
    for b in range(blocks):
        ret_ref[b * size:(b + 1) * size, :] = jnp.dot(
            perm, part_ref[b * size:(b + 1) * size, :], preferred_element_type=F32
        ).astype(BF)
        at = pl.ds(b * size, size)
        stores.append(pltpu.make_async_copy(ret_ref.at[at, :], ret_hbm.at[at, :], out_sems.at[b]))
        stores[-1].start()
    for store in stores:
        store.wait()


def down_kernel(hidden_ref, scaled_ref, down_hbm, down_ref, sems):
    step = 512
    stores = []
    for j in range(scaled_ref.shape[1] // step):
        at = slice(j * step, (j + 1) * step)
        down_ref[:, at] = lax.dot_general(
            hidden_ref[...], scaled_ref[:, at], TN, preferred_element_type=F32
        ).astype(BF)
        cols = pl.ds(j * step, step)
        stores.append(pltpu.make_async_copy(down_ref.at[:, cols], down_hbm.at[:, cols], sems.at[j]))
        stores[-1].start()
    for store in stores:
        store.wait()


def gate_kernel(experts, cap, me_ref, routes_ref, gates_ref, dots_ref, gate_grad_ref, gather_ref):
    toks = routes_ref.shape[1]
    rows = 4 * cap
    keys, first, second = slot_keys(routes_ref, experts)
    dots = dots_ref[...]
    lane = iota(dots.shape, 1) - me_ref[0] * cap
    mine = jnp.zeros((experts, toks), F32)
    for s in range(cap):
        column = jnp.sum(jnp.where(lane == s, dots, 0.0), axis=1, keepdims=True)
        mine = mine + jnp.where(keys == float(s), column, 0.0)
    gates = gates_ref[...].astype(F32)
    one = jnp.sum(jnp.where(first, mine, 0.0), axis=0, keepdims=True) / gates[0:1, :]
    two = jnp.sum(jnp.where(second, mine, 0.0), axis=0, keepdims=True) / gates[1:2, :]
    gate_grad_ref[...] = jnp.concatenate([one, two], axis=0).astype(BF)
    q = iota((experts, rows, toks), 1)
    value = jnp.where(keys[:, None, :] == (q % cap).astype(F32), 1.0, 0.0)
    for c in range(4):
        piece = jnp.where(q // cap == c, value, 0.0).reshape(experts * rows, toks)
        gather_ref[c * toks:(c + 1) * toks, :] = piece.T.astype(BF)


def combine_kernel(gather_ref, back_ref, token_grad_ref):
    toks = token_grad_ref.shape[0]
    wide = back_ref.shape[1]
    for c in range(4):
        token_grad_ref[:, c * wide:(c + 1) * wide] = jnp.dot(
            gather_ref[c * toks:(c + 1) * toks, :], back_ref[...], preferred_element_type=F32
        ).astype(BF)


VMEM = pl.BlockSpec(memory_space=pltpu.VMEM)
SMEM = pl.BlockSpec(memory_space=pltpu.SMEM)
HBM = pl.BlockSpec(memory_space=pltpu.HBM)


def call(kernel, ins, outs, scratch=(), limit=16, flops=0, moved=0):
    return pl.pallas_call(
        kernel,
        out_shape=tuple(jax.ShapeDtypeStruct(shape, kind) for shape, kind, _ in outs),
        in_specs=list(ins),
        out_specs=tuple(spec for _, _, spec in outs),
        scratch_shapes=list(scratch),
        compiler_params=pltpu.CompilerParams(vmem_limit_bytes=limit * 1024 * 1024),
        cost_estimate=pl.CostEstimate(flops=flops, bytes_accessed=moved, transcendentals=0),
    )


def local(tokens, routes, route_gates, out_grad, w_gate, w_up, w_down):
    experts = w_gate.shape[0] * lax.axis_size("expert")
    toks, fan_out = routes.shape
    dim = tokens.shape[1]
    hid = w_gate.shape[2]
    cap = 3 * toks * fan_out // (2 * experts)
    slots = experts * cap
    routes_t = routes.T
    gates_t = route_gates.T
    wd_full = lax.all_gather(w_down[0], "dp", axis=0, tiled=True)
    wgu = lax.all_gather(jnp.concatenate([w_gate[0], w_up[0]], axis=1), "dp", axis=0, tiled=True)

    (send,) = call(
        functools.partial(dispatch_kernel, experts, cap),
        (VMEM, VMEM, HBM, HBM),
        [((4 * slots, dim // 2), BF, HBM)],
        [
            pltpu.VMEM((4 * toks, dim // 2), BF), pltpu.VMEM((4 * slots, dim // 2), BF),
            pltpu.SemaphoreType.DMA((4,)), pltpu.SemaphoreType.DMA((experts // 16,)),
        ],
        limit=63, flops=2 * 4 * slots * 4 * toks * dim // 2, moved=8 * slots * dim,
    )(routes_t, gates_t, tokens, out_grad)
    recv = lax.all_to_all(
        send.reshape(experts, 4 * cap, dim // 2), "expert", split_axis=0, concat_axis=0, tiled=True
    ).reshape(4 * slots, dim // 2)

    ret, hidden, scaled, dots = call(
        functools.partial(expert_kernel, cap),
        (HBM, HBM, HBM),
        [
            ((4 * slots, dim // 4), BF, HBM), ((slots, hid), BF, VMEM), ((slots, dim), BF, VMEM),
            ((1, slots), F32, VMEM),
        ],
        [
            pltpu.VMEM((4 * slots, dim // 2), BF), pltpu.VMEM((dim, 2 * hid), BF), pltpu.VMEM((hid, dim), BF), pltpu.VMEM((slots, dim), BF),
            pltpu.VMEM((slots, 2 * hid), BF), pltpu.VMEM((4 * slots, dim // 4), BF),
            pltpu.VMEM((4 * slots, dim // 4), BF),
            pltpu.SemaphoreType.DMA((2,)), pltpu.SemaphoreType.DMA((experts // 16,)),
            pltpu.SemaphoreType.DMA((experts // 16,)),
        ],
        limit=62, flops=10 * slots * dim * hid, moved=16 * slots * dim,
    )(recv, wgu, wd_full)
    dots_all = lax.all_gather(dots, "expert", axis=0, tiled=True)
    back = lax.all_to_all(
        ret.reshape(experts, 4 * cap, dim // 4), "expert", split_axis=0, concat_axis=0, tiled=True
    ).reshape(4 * slots, dim // 4)
    (down,) = call(
        down_kernel, (VMEM, VMEM),
        [((hid, dim), BF, HBM)],
        [pltpu.VMEM((hid, dim), BF), pltpu.SemaphoreType.DMA((dim // 512,))],
        flops=2 * slots * dim * hid, moved=4 * slots * dim,
    )(hidden, scaled)
    down_grad = lax.psum_scatter(down, "dp", scatter_dimension=0, tiled=True)[None]
    me = lax.axis_index("expert").astype(jnp.int32).reshape(1)
    gate_grad, gather = call(
        functools.partial(gate_kernel, experts, cap),
        (SMEM, VMEM, VMEM, VMEM),
        [((fan_out, toks), BF, VMEM), ((4 * toks, 4 * slots), BF, VMEM)],
        limit=24, flops=1000000, moved=4 * slots * dim,
    )(me, routes_t, gates_t, dots_all)
    (token_grad,) = call(
        combine_kernel, (VMEM, VMEM),
        [((toks, dim), BF, VMEM)],
        flops=2 * 4 * toks * 4 * slots * dim // 4, moved=4 * slots * dim,
    )(gather, back)
    return token_grad, gate_grad.T, down_grad


def solution(mesh):
    rows = P(("dp", "expert"), None)
    weights = P("expert", "dp", None)
    return jax.shard_map(
        local,
        mesh=mesh,
        in_specs=(rows, rows, rows, rows, weights, weights, weights),
        out_specs=(rows, rows, weights),
        check_vma=False,
    )
```

```python
import functools

import jax
import jax.numpy as jnp
from jax import lax
from jax.experimental import pallas as pl
from jax.experimental.pallas import tpu as pltpu
from jax.sharding import PartitionSpec as P

BF = jnp.bfloat16
F32 = jnp.float32
NT = (((1,), (1,)), ((), ()))
TN = (((0,), (0,)), ((), ()))


def iota(shape, axis):
    return lax.broadcasted_iota(jnp.int32, shape, axis)


def slot_keys(routes_ref, experts):
    toks = routes_ref.shape[1]
    rows = iota((experts, toks), 0)
    first = routes_ref[0:1, :] == rows
    second = routes_ref[1:2, :] == rows
    named = jnp.where(first, 1.0, jnp.where(second, 1.0, 0.0))
    earlier = jnp.where(iota((toks, toks), 0) < iota((toks, toks), 1), 1.0, 0.0).astype(BF)
    before = jnp.dot(named.astype(BF), earlier, preferred_element_type=F32)
    return jnp.where(named > 0.5, before, -1.0), first, second


ROWS = 8
CHUNKS = 3


def tail_slot(p, q, cap):
    return (p - cap) * CHUNKS + q


def dispatch_kernel(
    experts, cap, routes_ref, gates_ref, tokens_ref, grads_ref, send_ref, tok_ref, grad_ref, out_ref, in_sems, out_sems
):
    toks, dim = tokens_ref.shape
    wide = dim // (CHUNKS + 1)
    loads = []
    for a, (src, dst) in enumerate(((tokens_ref, tok_ref), (grads_ref, grad_ref))):
        loads.append(pltpu.make_async_copy(src, dst, in_sems.at[a]))
        loads[-1].start()
    keys, first, second = slot_keys(routes_ref, experts)
    gates = gates_ref[...].astype(F32)
    gate = jnp.where(first, gates[0:1, :], jnp.where(second, gates[1:2, :], 0.0))
    block = 16
    size = block * ROWS
    p = iota((block, ROWS, toks), 1)
    main_slot = jnp.where(p < cap, p, -2).astype(F32)
    tail_slots = [jnp.where(p < cap, -2, tail_slot(p, q, cap)).astype(F32) for q in range(CHUNKS)]
    for load in loads:
        load.wait()
    stores = []
    for b in range(experts // block):
        key = keys[b * block:(b + 1) * block][:, None, :]
        g = gate[b * block:(b + 1) * block][:, None, :]
        hits = [jnp.where(key == slot, 1.0, 0.0) for slot in [main_slot] + tail_slots]
        plain = [hit.reshape(size, toks).astype(BF) for hit in hits]
        gated = [(hit * g).reshape(size, toks).astype(BF) for hit in hits]
        at = pl.ds(b * 2 * size, 2 * size)
        for q in range(CHUNKS):
            cols = slice(q * wide, (q + 1) * wide)
            both = []
            for ref, placing in ((tok_ref, plain), (grad_ref, gated)):
                lhs = jnp.concatenate([placing[0], placing[1 + q]], axis=1)
                rhs = jnp.concatenate([ref[:, cols], ref[:, CHUNKS * wide:]], axis=0)
                both.append(jnp.dot(lhs, rhs, preferred_element_type=F32).reshape(block, ROWS, wide))
            out_ref[b * 2 * size:(b + 1) * 2 * size, cols] = (
                jnp.concatenate(both, axis=1).reshape(2 * size, wide).astype(BF)
            )
        stores.append(pltpu.make_async_copy(out_ref.at[at, :], send_ref.at[at, :], out_sems.at[b]))
        stores[-1].start()
    for store in stores:
        store.wait()


def expert_kernel(
    cap, recv_hbm, wgu_hbm, wd_hbm, ret_hbm, down_hbm,
    recv_ref, wgu_ref, wd_ref, x_ref, scaled_ref, ggu_ref, part_ref, ret_ref, down_ref,
    in_sems, recv_sems, out_sems, down_sems,
):
    hid, dim = wd_ref.shape
    wide = dim // (CHUNKS + 1)
    tail = CHUNKS * wide
    block = 16
    size = 2 * block * ROWS
    count = block * cap
    blocks = recv_ref.shape[0] // size
    loads = []
    for b in range(blocks):
        at = pl.ds(b * size, size)
        loads.append(pltpu.make_async_copy(recv_hbm.at[at, :], recv_ref.at[at, :], recv_sems.at[b]))
        loads[-1].start()
    load_down = pltpu.make_async_copy(wd_hbm, wd_ref, in_sems.at[0])
    load_wgu = pltpu.make_async_copy(wgu_hbm, wgu_ref, in_sems.at[1])
    load_down.start()
    load_wgu.start()
    out_row = iota((count, 1), 0)
    in_row = iota((count, size), 1)
    source, slot = out_row // cap, out_row % cap

    def unpack(a, q):
        row = slot if q is None else jnp.where(slot % CHUNKS == q, cap + slot // CHUNKS, -size)
        return jnp.where(source * (2 * ROWS) + a * ROWS + row == in_row, 1.0, 0.0).astype(BF)

    mains = [unpack(0, None), unpack(1, None)]
    perms = [jnp.concatenate(mains + [unpack(0, q), unpack(1, q)], axis=0) for q in range(CHUNKS)]
    for b in range(blocks):
        loads[b].wait()
        at = slice(b * count, (b + 1) * count)
        tails = None
        for q in range(CHUNKS):
            cols = slice(q * wide, (q + 1) * wide)
            moved = jnp.dot(perms[q], recv_ref[b * size:(b + 1) * size, cols], preferred_element_type=F32)
            x_ref[at, cols] = moved[:count].astype(BF)
            scaled_ref[at, cols] = moved[count:2 * count].astype(BF)
            tails = moved[2 * count:] if tails is None else tails + moved[2 * count:]
        x_ref[at, tail:] = tails[:count].astype(BF)
        scaled_ref[at, tail:] = tails[count:].astype(BF)
    load_down.wait()
    hidden_grad = lax.dot_general(scaled_ref[...], wd_ref[...], NT, preferred_element_type=F32)
    load_wgu.wait()
    pre_gate = jnp.dot(x_ref[...], wgu_ref[:, :hid], preferred_element_type=F32)
    pre_up = jnp.dot(x_ref[...], wgu_ref[:, hid:], preferred_element_type=F32)
    squash = jax.nn.sigmoid(pre_gate)
    activated = pre_gate * squash
    hidden = (activated * pre_up).astype(BF)
    ggu_ref[:, :hid] = (hidden_grad * pre_up * squash * (1.0 + pre_gate * (1.0 - squash))).astype(BF)
    ggu_ref[:, hid:] = (hidden_grad * activated).astype(BF)
    dots = jnp.sum(hidden.astype(F32) * hidden_grad, axis=1, keepdims=True)
    high = dots.astype(BF).astype(F32)
    lane = iota((dots.shape[0], 128), 1)
    pair = jnp.where(lane == 0, high, jnp.where(lane == 1, dots - high, 0.0)).astype(BF)
    stores = []
    for q in range(CHUNKS + 1):
        cols = pl.ds(q * wide, wide)
        at = slice(q * wide, (q + 1) * wide)
        down_ref[:, at] = lax.dot_general(hidden, scaled_ref[:, at], TN, preferred_element_type=F32).astype(BF)
        stores.append(pltpu.make_async_copy(down_ref.at[:, cols], down_hbm.at[:, cols], down_sems.at[q]))
        stores[-1].start()
    for q in range(CHUNKS + 1):
        at = slice(q * wide, (q + 1) * wide)
        part_ref[:, at] = lax.dot_general(
            ggu_ref[...], wgu_ref[at, :], NT, preferred_element_type=F32
        ).astype(BF)
    size = block * ROWS
    out_row = iota((size, 1), 0)
    in_row = iota((size, count), 1)
    source, p = out_row // ROWS, out_row % ROWS

    def pack(q):
        slot = jnp.where(p < cap, p, -count) if q is None else jnp.where(p < cap, -count, tail_slot(p, q, cap))
        return jnp.where(source * cap + slot == in_row, 1.0, 0.0).astype(BF)

    main = pack(None)
    perms = [jnp.concatenate([main, pack(q)], axis=1) for q in range(CHUNKS)]
    for b in range(blocks):
        at = slice(b * count, (b + 1) * count)
        out = slice(b * size, (b + 1) * size)
        for q in range(CHUNKS):
            cols = slice(q * wide, (q + 1) * wide)
            rhs = jnp.concatenate([part_ref[at, cols], part_ref[at, tail:]], axis=0)
            ret_ref[out, cols] = jnp.dot(perms[q], rhs, preferred_element_type=F32).astype(BF)
        ret_ref[out, tail:] = jnp.dot(main, pair[at], preferred_element_type=F32).astype(BF)
        rows = pl.ds(b * size, size)
        stores.append(pltpu.make_async_copy(ret_ref.at[rows, :], ret_hbm.at[rows, :], out_sems.at[b]))
        stores[-1].start()
    for store in stores:
        store.wait()


def gather_kernel(experts, cap, routes_ref, after_ref, gather_ref):
    toks = routes_ref.shape[1]
    keys, first, second = slot_keys(routes_ref, experts)
    p = iota((experts, ROWS, toks), 1)
    main_slot = jnp.where(p < cap, p, -2).astype(F32)
    slots = [main_slot] + [jnp.where(p < cap, -2, tail_slot(p, q, cap)).astype(F32) for q in range(CHUNKS)]
    pieces = [(keys, slot) for slot in slots]
    pieces += [(jnp.where(choice, keys, -1.0), main_slot) for choice in (first, second)]
    for i, (key, slot) in enumerate(pieces):
        piece = jnp.where(key[:, None, :] == slot, 1.0, 0.0).reshape(experts * ROWS, toks)
        gather_ref[i * toks:(i + 1) * toks, :] = piece.T.astype(BF)


def combine_kernel(gates_ref, gather_ref, back_ref, token_grad_ref, gate_grad_ref):
    toks, dim = token_grad_ref.shape
    wide = dim // (CHUNKS + 1)
    tail = CHUNKS * wide
    tails = None
    for q in range(CHUNKS):
        cols = slice(q * wide, (q + 1) * wide)
        lhs = jnp.concatenate([gather_ref[:toks, :], gather_ref[(1 + q) * toks:(2 + q) * toks, :]], axis=0)
        moved = jnp.dot(lhs, back_ref[:, cols], preferred_element_type=F32)
        token_grad_ref[:, cols] = moved[:toks].astype(BF)
        tails = moved[toks:] if tails is None else tails + moved[toks:]
    token_grad_ref[:, tail:] = tails.astype(BF)
    dots = jnp.dot(gather_ref[(1 + CHUNKS) * toks:, :], back_ref[:, tail:], preferred_element_type=F32)
    gates = gates_ref[...].astype(F32)
    rows = []
    for k in range(2):
        pair = dots[k * toks:(k + 1) * toks].T
        rows.append((pair[0:1] + pair[1:2]) / gates[k:k + 1])
    gate_grad_ref[...] = jnp.concatenate(rows, axis=0).astype(BF)


VMEM = pl.BlockSpec(memory_space=pltpu.VMEM)
SMEM = pl.BlockSpec(memory_space=pltpu.SMEM)
HBM = pl.BlockSpec(memory_space=pltpu.HBM)


def call(kernel, ins, outs, scratch=(), limit=16, flops=0, moved=0):
    return pl.pallas_call(
        kernel,
        out_shape=tuple(jax.ShapeDtypeStruct(shape, kind) for shape, kind, _ in outs),
        in_specs=list(ins),
        out_specs=tuple(spec for _, _, spec in outs),
        scratch_shapes=list(scratch),
        compiler_params=pltpu.CompilerParams(vmem_limit_bytes=limit * 1024 * 1024),
        cost_estimate=pl.CostEstimate(flops=flops, bytes_accessed=moved, transcendentals=0),
    )


def local(tokens, routes, route_gates, out_grad, w_gate, w_up, w_down):
    experts = w_gate.shape[0] * lax.axis_size("expert")
    toks, fan_out = routes.shape
    dim = tokens.shape[1]
    hid = w_gate.shape[2]
    cap = 3 * toks * fan_out // (2 * experts)
    slots = experts * cap
    main = CHUNKS * dim // (CHUNKS + 1)
    packed = experts * ROWS
    DMA = pltpu.SemaphoreType.DMA
    routes_t = routes.T
    gates_t = route_gates.T
    wd_full = lax.all_gather(w_down[0], "dp", axis=0, tiled=True)
    wgu = lax.all_gather(jnp.concatenate([w_gate[0], w_up[0]], axis=1), "dp", axis=0, tiled=True)

    (send,) = call(
        functools.partial(dispatch_kernel, experts, cap),
        (VMEM, VMEM, HBM, HBM),
        [((2 * packed, main), BF, HBM)],
        [
            pltpu.VMEM((toks, dim), BF), pltpu.VMEM((toks, dim), BF), pltpu.VMEM((2 * packed, main), BF),
            DMA((2,)), DMA((experts // 16,)),
        ],
        limit=63, flops=8 * packed * toks * main, moved=4 * packed * main,
    )(routes_t, gates_t, tokens, out_grad)
    recv = lax.all_to_all(
        send.reshape(experts, 2 * ROWS, main), "expert", split_axis=0, concat_axis=0, tiled=True
    ).reshape(2 * packed, main)

    ret, down = call(
        functools.partial(expert_kernel, cap),
        (HBM, HBM, HBM),
        [((packed, main + 128), BF, HBM), ((hid, dim), BF, HBM)],
        [
            pltpu.VMEM((2 * packed, main), BF), pltpu.VMEM((dim, 2 * hid), BF), pltpu.VMEM((hid, dim), BF),
            pltpu.VMEM((slots, dim), BF), pltpu.VMEM((slots, dim), BF), pltpu.VMEM((slots, 2 * hid), BF),
            pltpu.VMEM((slots, dim), BF), pltpu.VMEM((packed, main + 128), BF), pltpu.VMEM((hid, dim), BF),
            DMA((2,)), DMA((experts // 16,)), DMA((experts // 16,)), DMA((CHUNKS + 1,)),
        ],
        limit=62, flops=12 * slots * dim * hid, moved=16 * slots * dim,
    )(recv, wgu, wd_full)
    down_grad = lax.psum_scatter(down, "dp", scatter_dimension=0, tiled=True)[None]
    back = lax.all_to_all(
        ret.reshape(experts, ROWS, main + 128), "expert", split_axis=0, concat_axis=0, tiled=True
    ).reshape(packed, main + 128)
    (gather,) = call(
        functools.partial(gather_kernel, experts, cap),
        (VMEM, HBM),
        [(((3 + CHUNKS) * toks, packed), BF, VMEM)],
        limit=62, flops=1000000, moved=12 * toks * packed,
    )(routes_t, wd_full)
    token_grad, gate_grad = call(
        combine_kernel, (VMEM, VMEM, VMEM),
        [((toks, dim), BF, VMEM), ((fan_out, toks), BF, VMEM)],
        flops=4 * toks * packed * dim, moved=4 * packed * dim,
    )(gates_t, gather, back)
    return token_grad, gate_grad.T, down_grad


def solution(mesh):
    rows = P(("dp", "expert"), None)
    weights = P("expert", "dp", None)
    return jax.shard_map(
        local,
        mesh=mesh,
        in_specs=(rows, rows, rows, rows, weights, weights, weights),
        out_specs=(rows, rows, weights),
        check_vma=False,
    )
```

```python
import functools

import jax
import jax.numpy as jnp
from jax import lax
from jax.experimental import pallas as pl
from jax.experimental.pallas import tpu as pltpu
from jax.sharding import PartitionSpec as P

BF = jnp.bfloat16
F32 = jnp.float32
NT = (((1,), (1,)), ((), ()))
TN = (((0,), (0,)), ((), ()))


def iota(shape, axis):
    return lax.broadcasted_iota(jnp.int32, shape, axis)


def slot_keys(routes_ref, experts):
    toks = routes_ref.shape[1]
    rows = iota((experts, toks), 0)
    first = routes_ref[0:1, :] == rows
    second = routes_ref[1:2, :] == rows
    named = jnp.where(first, 1.0, jnp.where(second, 1.0, 0.0))
    earlier = jnp.where(iota((toks, toks), 0) < iota((toks, toks), 1), 1.0, 0.0).astype(BF)
    before = jnp.dot(named.astype(BF), earlier, preferred_element_type=F32)
    return jnp.where(named > 0.5, before, -1.0), first, second


ROWS = 8
CHUNKS = 3


def tail_slot(p, q, cap):
    return (p - cap) * CHUNKS + q


def dispatch_kernel(
    experts, cap, routes_ref, gates_ref, tokens_ref, grads_ref, send_ref, tok_ref, grad_ref, out_ref, in_sems, out_sems
):
    toks, dim = tokens_ref.shape
    wide = dim // (CHUNKS + 1)
    loads = []
    for a, (src, dst) in enumerate(((tokens_ref, tok_ref), (grads_ref, grad_ref))):
        loads.append(pltpu.make_async_copy(src, dst, in_sems.at[a]))
        loads[-1].start()
    keys, first, second = slot_keys(routes_ref, experts)
    gates = gates_ref[...].astype(F32)
    gate = jnp.where(first, gates[0:1, :], jnp.where(second, gates[1:2, :], 0.0))
    block = 16
    size = block * ROWS
    p = iota((block, ROWS, toks), 1)
    main_slot = jnp.where(p < cap, p, -2).astype(F32)
    tail_slots = [jnp.where(p < cap, -2, tail_slot(p, q, cap)).astype(F32) for q in range(CHUNKS)]
    for load in loads:
        load.wait()
    stores = []
    for b in range(experts // block):
        key = keys[b * block:(b + 1) * block][:, None, :]
        g = gate[b * block:(b + 1) * block][:, None, :]
        hits = [jnp.where(key == slot, 1.0, 0.0) for slot in [main_slot] + tail_slots]
        plain = [hit.reshape(size, toks).astype(BF) for hit in hits]
        gated = [(hit * g).reshape(size, toks).astype(BF) for hit in hits]
        at = pl.ds(b * 2 * size, 2 * size)
        for q in range(CHUNKS):
            cols = slice(q * wide, (q + 1) * wide)
            both = []
            for ref, placing in ((tok_ref, plain), (grad_ref, gated)):
                lhs = jnp.concatenate([placing[0], placing[1 + q]], axis=1)
                rhs = jnp.concatenate([ref[:, cols], ref[:, CHUNKS * wide:]], axis=0)
                both.append(jnp.dot(lhs, rhs, preferred_element_type=F32).reshape(block, ROWS, wide))
            out_ref[b * 2 * size:(b + 1) * 2 * size, cols] = (
                jnp.concatenate(both, axis=1).reshape(2 * size, wide).astype(BF)
            )
        stores.append(pltpu.make_async_copy(out_ref.at[at, :], send_ref.at[at, :], out_sems.at[b]))
        stores[-1].start()
    for store in stores:
        store.wait()


def expert_kernel(
    cap, recv_hbm, wgu_hbm, ret_hbm, down_hbm,
    recv_ref, wgu_ref, wd_ref, x_ref, scaled_ref, ggu_ref, part_ref, ret_ref, down_ref,
    in_sems, recv_sems, out_sems, down_sems,
):
    hid, dim = wd_ref.shape
    wide = dim // (CHUNKS + 1)
    tail = CHUNKS * wide
    block = 16
    size = 2 * block * ROWS
    count = block * cap
    blocks = recv_ref.shape[0] // size
    loads = []
    for b in range(blocks):
        at = pl.ds(b * size, size)
        loads.append(pltpu.make_async_copy(recv_hbm.at[at, :], recv_ref.at[at, :], recv_sems.at[b]))
        loads[-1].start()
    load_wgu = pltpu.make_async_copy(wgu_hbm, wgu_ref, in_sems.at[0])
    load_wgu.start()
    out_row = iota((count, 1), 0)
    in_row = iota((count, size), 1)
    source, slot = out_row // cap, out_row % cap

    def unpack(a, q):
        row = slot if q is None else jnp.where(slot % CHUNKS == q, cap + slot // CHUNKS, -size)
        return jnp.where(source * (2 * ROWS) + a * ROWS + row == in_row, 1.0, 0.0).astype(BF)

    mains = [unpack(0, None), unpack(1, None)]
    perms = [jnp.concatenate(mains + [unpack(0, q), unpack(1, q)], axis=0) for q in range(CHUNKS)]
    for b in range(blocks):
        loads[b].wait()
        at = slice(b * count, (b + 1) * count)
        tails = None
        for q in range(CHUNKS):
            cols = slice(q * wide, (q + 1) * wide)
            moved = jnp.dot(perms[q], recv_ref[b * size:(b + 1) * size, cols], preferred_element_type=F32)
            x_ref[at, cols] = moved[:count].astype(BF)
            scaled_ref[at, cols] = moved[count:2 * count].astype(BF)
            tails = moved[2 * count:] if tails is None else tails + moved[2 * count:]
        x_ref[at, tail:] = tails[:count].astype(BF)
        scaled_ref[at, tail:] = tails[count:].astype(BF)
    load_wgu.wait()
    unpack_down(wgu_ref, wd_ref)
    hidden_grad = lax.dot_general(scaled_ref[...], wd_ref[...], NT, preferred_element_type=F32)
    pre_gate = jnp.dot(x_ref[...], wgu_ref[:, :hid], preferred_element_type=F32)
    pre_up = jnp.dot(x_ref[...], wgu_ref[:, hid:2 * hid], preferred_element_type=F32)
    squash = jax.nn.sigmoid(pre_gate)
    activated = pre_gate * squash
    hidden = (activated * pre_up).astype(BF)
    ggu_ref[:, :hid] = (hidden_grad * pre_up * squash * (1.0 + pre_gate * (1.0 - squash))).astype(BF)
    ggu_ref[:, hid:] = (hidden_grad * activated).astype(BF)
    dots = jnp.sum(hidden.astype(F32) * hidden_grad, axis=1, keepdims=True)
    high = dots.astype(BF).astype(F32)
    lane = iota((dots.shape[0], 128), 1)
    pair = jnp.where(lane == 0, high, jnp.where(lane == 1, dots - high, 0.0)).astype(BF)
    stores = []
    for q in range(CHUNKS + 1):
        cols = pl.ds(q * wide, wide)
        at = slice(q * wide, (q + 1) * wide)
        down_ref[:, at] = lax.dot_general(hidden, scaled_ref[:, at], TN, preferred_element_type=F32).astype(BF)
        stores.append(pltpu.make_async_copy(down_ref.at[:, cols], down_hbm.at[:, cols], down_sems.at[q]))
        stores[-1].start()
    for q in range(CHUNKS + 1):
        at = slice(q * wide, (q + 1) * wide)
        part_ref[:, at] = lax.dot_general(
            ggu_ref[...], wgu_ref[at, :2 * hid], NT, preferred_element_type=F32
        ).astype(BF)
    size = block * ROWS
    out_row = iota((size, 1), 0)
    in_row = iota((size, count), 1)
    source, p = out_row // ROWS, out_row % ROWS

    def pack(q):
        slot = jnp.where(p < cap, p, -count) if q is None else jnp.where(p < cap, -count, tail_slot(p, q, cap))
        return jnp.where(source * cap + slot == in_row, 1.0, 0.0).astype(BF)

    main = pack(None)
    perms = [jnp.concatenate([main, pack(q)], axis=1) for q in range(CHUNKS)]
    for b in range(blocks):
        at = slice(b * count, (b + 1) * count)
        out = slice(b * size, (b + 1) * size)
        for q in range(CHUNKS):
            cols = slice(q * wide, (q + 1) * wide)
            rhs = jnp.concatenate([part_ref[at, cols], part_ref[at, tail:]], axis=0)
            ret_ref[out, cols] = jnp.dot(perms[q], rhs, preferred_element_type=F32).astype(BF)
        ret_ref[out, tail:] = jnp.dot(main, pair[at], preferred_element_type=F32).astype(BF)
        rows = pl.ds(b * size, size)
        stores.append(pltpu.make_async_copy(ret_ref.at[rows, :], ret_hbm.at[rows, :], out_sems.at[b]))
        stores[-1].start()
    for store in stores:
        store.wait()


def pack_kernel(gate_ref, up_ref, down_ref, out_ref):
    hid = gate_ref.shape[1]
    out_ref[:, :hid] = gate_ref[...]
    out_ref[:, hid:2 * hid] = up_ref[...]
    for r in range(down_ref.shape[0] // 16):
        for l in range(down_ref.shape[1] // 128):
            out_ref[l * 16:(l + 1) * 16, 2 * hid + r * 128:2 * hid + (r + 1) * 128] = (
                down_ref[r * 16:(r + 1) * 16, l * 128:(l + 1) * 128]
            )


def unpack_down(packed_ref, down_ref):
    hid, dim = down_ref.shape
    lanes = packed_ref.shape[1] - hid
    high = 16 * (dim // 128)
    each = hid * high // packed_ref.shape[0]
    for part in range(packed_ref.shape[0] // high):
        for r in range(each // 16):
            for l in range(dim // 128):
                down_ref[part * each + r * 16:part * each + (r + 1) * 16, l * 128:(l + 1) * 128] = packed_ref[
                    part * high + l * 16:part * high + (l + 1) * 16, lanes + r * 128:lanes + (r + 1) * 128
                ]


def gather_kernel(experts, cap, routes_ref, after_ref, gather_ref):
    toks = routes_ref.shape[1]
    keys, first, second = slot_keys(routes_ref, experts)
    p = iota((experts, ROWS, toks), 1)
    main_slot = jnp.where(p < cap, p, -2).astype(F32)
    slots = [main_slot] + [jnp.where(p < cap, -2, tail_slot(p, q, cap)).astype(F32) for q in range(CHUNKS)]
    pieces = [(keys, slot) for slot in slots]
    pieces += [(jnp.where(choice, keys, -1.0), main_slot) for choice in (first, second)]
    for i, (key, slot) in enumerate(pieces):
        piece = jnp.where(key[:, None, :] == slot, 1.0, 0.0).reshape(experts * ROWS, toks)
        gather_ref[i * toks:(i + 1) * toks, :] = piece.T.astype(BF)


def combine_kernel(gates_ref, gather_ref, back_ref, token_grad_ref, gate_grad_ref):
    toks, dim = token_grad_ref.shape
    wide = dim // (CHUNKS + 1)
    tail = CHUNKS * wide
    tails = None
    for q in range(CHUNKS):
        cols = slice(q * wide, (q + 1) * wide)
        lhs = jnp.concatenate([gather_ref[:toks, :], gather_ref[(1 + q) * toks:(2 + q) * toks, :]], axis=0)
        moved = jnp.dot(lhs, back_ref[:, cols], preferred_element_type=F32)
        token_grad_ref[:, cols] = moved[:toks].astype(BF)
        tails = moved[toks:] if tails is None else tails + moved[toks:]
    token_grad_ref[:, tail:] = tails.astype(BF)
    dots = jnp.dot(gather_ref[(1 + CHUNKS) * toks:, :], back_ref[:, tail:], preferred_element_type=F32)
    gates = gates_ref[...].astype(F32)
    rows = []
    for k in range(2):
        pair = dots[k * toks:(k + 1) * toks].T
        rows.append((pair[0:1] + pair[1:2]) / gates[k:k + 1])
    gate_grad_ref[...] = jnp.concatenate(rows, axis=0).astype(BF)


VMEM = pl.BlockSpec(memory_space=pltpu.VMEM)
SMEM = pl.BlockSpec(memory_space=pltpu.SMEM)
HBM = pl.BlockSpec(memory_space=pltpu.HBM)


def call(kernel, ins, outs, scratch=(), limit=16, flops=0, moved=0):
    return pl.pallas_call(
        kernel,
        out_shape=tuple(jax.ShapeDtypeStruct(shape, kind) for shape, kind, _ in outs),
        in_specs=list(ins),
        out_specs=tuple(spec for _, _, spec in outs),
        scratch_shapes=list(scratch),
        compiler_params=pltpu.CompilerParams(vmem_limit_bytes=limit * 1024 * 1024),
        cost_estimate=pl.CostEstimate(flops=flops, bytes_accessed=moved, transcendentals=0),
    )


def local(tokens, routes, route_gates, out_grad, w_gate, w_up, w_down):
    experts = w_gate.shape[0] * lax.axis_size("expert")
    toks, fan_out = routes.shape
    dim = tokens.shape[1]
    hid = w_gate.shape[2]
    cap = 3 * toks * fan_out // (2 * experts)
    slots = experts * cap
    main = CHUNKS * dim // (CHUNKS + 1)
    packed = experts * ROWS
    DMA = pltpu.SemaphoreType.DMA
    routes_t = routes.T
    gates_t = route_gates.T
    (mine,) = call(pack_kernel, (VMEM, VMEM, VMEM), [((dim // lax.axis_size("dp"), 3 * hid), BF, VMEM)])(
        w_gate[0], w_up[0], w_down[0]
    )
    weights = lax.all_gather(mine, "dp", axis=0, tiled=True)

    (send,) = call(
        functools.partial(dispatch_kernel, experts, cap),
        (VMEM, VMEM, HBM, HBM),
        [((2 * packed, main), BF, HBM)],
        [
            pltpu.VMEM((toks, dim), BF), pltpu.VMEM((toks, dim), BF), pltpu.VMEM((2 * packed, main), BF),
            DMA((2,)), DMA((experts // 16,)),
        ],
        limit=63, flops=8 * packed * toks * main, moved=4 * packed * main,
    )(routes_t, gates_t, tokens, out_grad)
    recv = lax.all_to_all(
        send.reshape(experts, 2 * ROWS, main), "expert", split_axis=0, concat_axis=0, tiled=True
    ).reshape(2 * packed, main)

    ret, down = call(
        functools.partial(expert_kernel, cap),
        (HBM, HBM),
        [((packed, main + 128), BF, HBM), ((hid, dim), BF, HBM)],
        [
            pltpu.VMEM((2 * packed, main), BF), pltpu.VMEM((dim, 3 * hid), BF), pltpu.VMEM((hid, dim), BF),
            pltpu.VMEM((slots, dim), BF), pltpu.VMEM((slots, dim), BF), pltpu.VMEM((slots, 2 * hid), BF),
            pltpu.VMEM((slots, dim), BF), pltpu.VMEM((packed, main + 128), BF), pltpu.VMEM((hid, dim), BF),
            DMA((1,)), DMA((experts // 16,)), DMA((experts // 16,)), DMA((CHUNKS + 1,)),
        ],
        limit=62, flops=12 * slots * dim * hid, moved=16 * slots * dim,
    )(recv, weights)
    down_grad = lax.psum_scatter(down, "dp", scatter_dimension=0, tiled=True)[None]
    back = lax.all_to_all(
        ret.reshape(experts, ROWS, main + 128), "expert", split_axis=0, concat_axis=0, tiled=True
    ).reshape(packed, main + 128)
    (gather,) = call(
        functools.partial(gather_kernel, experts, cap),
        (VMEM, HBM),
        [(((3 + CHUNKS) * toks, packed), BF, VMEM)],
        limit=62, flops=1000000, moved=12 * toks * packed,
    )(routes_t, weights)
    token_grad, gate_grad = call(
        combine_kernel, (VMEM, VMEM, VMEM),
        [((toks, dim), BF, VMEM), ((fan_out, toks), BF, VMEM)],
        flops=4 * toks * packed * dim, moved=4 * packed * dim,
    )(gates_t, gather, back)
    return token_grad, gate_grad.T, down_grad


def solution(mesh):
    rows = P(("dp", "expert"), None)
    weights = P("expert", "dp", None)
    return jax.shard_map(
        local,
        mesh=mesh,
        in_specs=(rows, rows, rows, rows, weights, weights, weights),
        out_specs=(rows, rows, weights),
        check_vma=False,
    )
```

```python
import functools

import jax
import jax.numpy as jnp
from jax import lax
from jax.experimental import pallas as pl
from jax.experimental.pallas import tpu as pltpu
from jax.sharding import PartitionSpec as P

BF = jnp.bfloat16
F32 = jnp.float32
NT = (((1,), (1,)), ((), ()))
TN = (((0,), (0,)), ((), ()))


def iota(shape, axis):
    return lax.broadcasted_iota(jnp.int32, shape, axis)


def slot_keys(routes_ref, experts):
    toks = routes_ref.shape[1]
    rows = iota((experts, toks), 0)
    first = routes_ref[0:1, :] == rows
    second = routes_ref[1:2, :] == rows
    named = jnp.where(first, 1.0, jnp.where(second, 1.0, 0.0))
    earlier = jnp.where(iota((toks, toks), 0) < iota((toks, toks), 1), 1.0, 0.0).astype(BF)
    before = jnp.dot(named.astype(BF), earlier, preferred_element_type=F32)
    return jnp.where(named > 0.5, before, -1.0), first, second


ROWS = 8
CHUNKS = 3


def tail_slot(p, q, cap):
    return (p - cap) * CHUNKS + q


def dispatch_kernel(
    experts, cap, routes_ref, gates_ref, tokens_ref, grads_ref, gate_hbm, up_hbm, down_hbm, send_ref, weights_hbm,
    tok_ref, grad_ref, out_ref, down_ref, pack_ref, in_sems, out_sems, weight_sems,
):
    toks, dim = tokens_ref.shape
    wide = dim // (CHUNKS + 1)
    hid = gate_hbm.shape[1]
    load_down = pltpu.make_async_copy(down_hbm, down_ref, weight_sems.at[3])
    load_down.start()
    load_slices = []
    for i, src in enumerate((gate_hbm, up_hbm)):
        load_slices.append(pltpu.make_async_copy(src, pack_ref.at[:, pl.ds(i * hid, hid)], weight_sems.at[i]))
        load_slices[-1].start()
    loads = []
    for a, (src, dst) in enumerate(((tokens_ref, tok_ref), (grads_ref, grad_ref))):
        loads.append(pltpu.make_async_copy(src, dst, in_sems.at[a]))
        loads[-1].start()
    keys, first, second = slot_keys(routes_ref, experts)
    gates = gates_ref[...].astype(F32)
    gate = jnp.where(first, gates[0:1, :], jnp.where(second, gates[1:2, :], 0.0))
    block = 16
    size = block * ROWS
    p = iota((block, ROWS, toks), 1)
    main_slot = jnp.where(p < cap, p, -2).astype(F32)
    tail_slots = [jnp.where(p < cap, -2, tail_slot(p, q, cap)).astype(F32) for q in range(CHUNKS)]
    load_down.wait()
    for r in range(down_ref.shape[0] // 16):
        for l in range(dim // 128):
            pack_ref[l * 16:(l + 1) * 16, 2 * hid + r * 128:2 * hid + (r + 1) * 128] = (
                down_ref[r * 16:(r + 1) * 16, l * 128:(l + 1) * 128]
            )
    for load in load_slices:
        load.wait()
    stores = [pltpu.make_async_copy(pack_ref, weights_hbm, weight_sems.at[2])]
    stores[0].start()
    for load in loads:
        load.wait()
    for b in range(experts // block):
        key = keys[b * block:(b + 1) * block][:, None, :]
        g = gate[b * block:(b + 1) * block][:, None, :]
        hits = [jnp.where(key == slot, 1.0, 0.0) for slot in [main_slot] + tail_slots]
        plain = [hit.reshape(size, toks).astype(BF) for hit in hits]
        gated = [(hit * g).reshape(size, toks).astype(BF) for hit in hits]
        at = pl.ds(b * 2 * size, 2 * size)
        for q in range(CHUNKS):
            cols = slice(q * wide, (q + 1) * wide)
            both = []
            for ref, placing in ((tok_ref, plain), (grad_ref, gated)):
                lhs = jnp.concatenate([placing[0], placing[1 + q]], axis=1)
                rhs = jnp.concatenate([ref[:, cols], ref[:, CHUNKS * wide:]], axis=0)
                both.append(jnp.dot(lhs, rhs, preferred_element_type=F32).reshape(block, ROWS, wide))
            out_ref[b * 2 * size:(b + 1) * 2 * size, cols] = (
                jnp.concatenate(both, axis=1).reshape(2 * size, wide).astype(BF)
            )
        stores.append(pltpu.make_async_copy(out_ref.at[at, :], send_ref.at[at, :], out_sems.at[b]))
        stores[-1].start()
    for store in stores:
        store.wait()


def expert_kernel(
    cap, recv_hbm, wgu_hbm, ret_hbm, down_hbm,
    recv_ref, wgu_ref, wd_ref, x_ref, scaled_ref, ggu_ref, part_ref, ret_ref, down_ref,
    in_sems, recv_sems, out_sems, down_sems,
):
    hid, dim = wd_ref.shape
    wide = dim // (CHUNKS + 1)
    tail = CHUNKS * wide
    block = 16
    size = 2 * block * ROWS
    count = block * cap
    blocks = recv_ref.shape[0] // size
    loads = []
    for b in range(blocks):
        at = pl.ds(b * size, size)
        loads.append(pltpu.make_async_copy(recv_hbm.at[at, :], recv_ref.at[at, :], recv_sems.at[b]))
        loads[-1].start()
    load_wgu = pltpu.make_async_copy(wgu_hbm, wgu_ref, in_sems.at[0])
    load_wgu.start()
    out_row = iota((count, 1), 0)
    in_row = iota((count, size), 1)
    source, slot = out_row // cap, out_row % cap

    def unpack(a, q):
        row = slot if q is None else jnp.where(slot % CHUNKS == q, cap + slot // CHUNKS, -size)
        return jnp.where(source * (2 * ROWS) + a * ROWS + row == in_row, 1.0, 0.0).astype(BF)

    mains = [unpack(0, None), unpack(1, None)]
    perms = [jnp.concatenate(mains + [unpack(0, q), unpack(1, q)], axis=0) for q in range(CHUNKS)]
    for b in range(blocks):
        loads[b].wait()
        at = slice(b * count, (b + 1) * count)
        tails = None
        for q in range(CHUNKS):
            cols = slice(q * wide, (q + 1) * wide)
            moved = jnp.dot(perms[q], recv_ref[b * size:(b + 1) * size, cols], preferred_element_type=F32)
            x_ref[at, cols] = moved[:count].astype(BF)
            scaled_ref[at, cols] = moved[count:2 * count].astype(BF)
            tails = moved[2 * count:] if tails is None else tails + moved[2 * count:]
        x_ref[at, tail:] = tails[:count].astype(BF)
        scaled_ref[at, tail:] = tails[count:].astype(BF)
    load_wgu.wait()
    unpack_down(wgu_ref, wd_ref)
    hidden_grad = lax.dot_general(scaled_ref[...], wd_ref[...], NT, preferred_element_type=F32)
    pre_gate = jnp.dot(x_ref[...], wgu_ref[:, :hid], preferred_element_type=F32)
    pre_up = jnp.dot(x_ref[...], wgu_ref[:, hid:2 * hid], preferred_element_type=F32)
    squash = jax.nn.sigmoid(pre_gate)
    activated = pre_gate * squash
    hidden = (activated * pre_up).astype(BF)
    ggu_ref[:, :hid] = (hidden_grad * pre_up * squash * (1.0 + pre_gate * (1.0 - squash))).astype(BF)
    ggu_ref[:, hid:] = (hidden_grad * activated).astype(BF)
    dots = jnp.sum(hidden.astype(F32) * hidden_grad, axis=1, keepdims=True)
    high = dots.astype(BF).astype(F32)
    lane = iota((dots.shape[0], 128), 1)
    pair = jnp.where(lane == 0, high, jnp.where(lane == 1, dots - high, 0.0)).astype(BF)
    stores = []
    for q in range(CHUNKS + 1):
        cols = pl.ds(q * wide, wide)
        at = slice(q * wide, (q + 1) * wide)
        down_ref[:, at] = lax.dot_general(hidden, scaled_ref[:, at], TN, preferred_element_type=F32).astype(BF)
        stores.append(pltpu.make_async_copy(down_ref.at[:, cols], down_hbm.at[:, cols], down_sems.at[q]))
        stores[-1].start()
    for q in range(CHUNKS + 1):
        at = slice(q * wide, (q + 1) * wide)
        part_ref[:, at] = lax.dot_general(
            ggu_ref[...], wgu_ref[at, :2 * hid], NT, preferred_element_type=F32
        ).astype(BF)
    size = block * ROWS
    out_row = iota((size, 1), 0)
    in_row = iota((size, count), 1)
    source, p = out_row // ROWS, out_row % ROWS

    def pack(q):
        slot = jnp.where(p < cap, p, -count) if q is None else jnp.where(p < cap, -count, tail_slot(p, q, cap))
        return jnp.where(source * cap + slot == in_row, 1.0, 0.0).astype(BF)

    main = pack(None)
    perms = [jnp.concatenate([main, pack(q)], axis=1) for q in range(CHUNKS)]
    for b in range(blocks):
        at = slice(b * count, (b + 1) * count)
        out = slice(b * size, (b + 1) * size)
        for q in range(CHUNKS):
            cols = slice(q * wide, (q + 1) * wide)
            rhs = jnp.concatenate([part_ref[at, cols], part_ref[at, tail:]], axis=0)
            ret_ref[out, cols] = jnp.dot(perms[q], rhs, preferred_element_type=F32).astype(BF)
        ret_ref[out, tail:] = jnp.dot(main, pair[at], preferred_element_type=F32).astype(BF)
        rows = pl.ds(b * size, size)
        stores.append(pltpu.make_async_copy(ret_ref.at[rows, :], ret_hbm.at[rows, :], out_sems.at[b]))
        stores[-1].start()
    for store in stores:
        store.wait()


def unpack_down(packed_ref, down_ref):
    hid, dim = down_ref.shape
    lanes = packed_ref.shape[1] - hid
    high = 16 * (dim // 128)
    each = hid * high // packed_ref.shape[0]
    for part in range(packed_ref.shape[0] // high):
        for r in range(each // 16):
            for l in range(dim // 128):
                down_ref[part * each + r * 16:part * each + (r + 1) * 16, l * 128:(l + 1) * 128] = packed_ref[
                    part * high + l * 16:part * high + (l + 1) * 16, lanes + r * 128:lanes + (r + 1) * 128
                ]


def combine_kernel(experts, cap, routes_ref, gates_ref, back_ref, after_ref, token_grad_ref, gate_grad_ref):
    toks, dim = token_grad_ref.shape
    wide = dim // (CHUNKS + 1)
    tail = CHUNKS * wide
    packed = experts * ROWS
    keys, first, _ = slot_keys(routes_ref, experts)
    spread = jnp.where(iota((experts, packed), 0) == iota((experts, packed), 1) // ROWS, 1.0, 0.0).astype(BF)
    key = lax.dot_general(keys.astype(BF), spread, TN, preferred_element_type=F32)
    one = lax.dot_general(jnp.where(first, 1.0, 0.0).astype(BF), spread, TN, preferred_element_type=F32)
    p = iota((1, packed), 1) % ROWS
    main_slot = jnp.where(p < cap, p, -2).astype(F32)
    main = jnp.where(key == main_slot, 1.0, 0.0)
    choices = jnp.concatenate([main * one, main * (1.0 - one)], axis=0).astype(BF)
    lhs = []
    for q in range(CHUNKS):
        slot = jnp.where(p < cap, -2, tail_slot(p, q, cap)).astype(F32)
        lhs.append(jnp.concatenate([main, jnp.where(key == slot, 1.0, 0.0)], axis=0).astype(BF))
    tails = None
    for q in range(CHUNKS):
        cols = slice(q * wide, (q + 1) * wide)
        moved = jnp.dot(lhs[q], back_ref[:, cols], preferred_element_type=F32)
        token_grad_ref[:, cols] = moved[:toks].astype(BF)
        tails = moved[toks:] if tails is None else tails + moved[toks:]
    token_grad_ref[:, tail:] = tails.astype(BF)
    dots = jnp.dot(choices, back_ref[:, tail:], preferred_element_type=F32)
    gates = gates_ref[...].astype(F32)
    rows = []
    for k in range(2):
        pair = dots[k * toks:(k + 1) * toks].T
        rows.append((pair[0:1] + pair[1:2]) / gates[k:k + 1])
    gate_grad_ref[...] = jnp.concatenate(rows, axis=0).astype(BF)


def after_kernel(down_ref, out_ref):
    out_ref[...] = jnp.zeros_like(out_ref)


VMEM = pl.BlockSpec(memory_space=pltpu.VMEM)
SMEM = pl.BlockSpec(memory_space=pltpu.SMEM)
HBM = pl.BlockSpec(memory_space=pltpu.HBM)


def call(kernel, ins, outs, scratch=(), limit=16, flops=0, moved=0):
    return pl.pallas_call(
        kernel,
        out_shape=tuple(jax.ShapeDtypeStruct(shape, kind) for shape, kind, _ in outs),
        in_specs=list(ins),
        out_specs=tuple(spec for _, _, spec in outs),
        scratch_shapes=list(scratch),
        compiler_params=pltpu.CompilerParams(vmem_limit_bytes=limit * 1024 * 1024),
        cost_estimate=pl.CostEstimate(flops=flops, bytes_accessed=moved, transcendentals=0),
    )


def local(tokens, routes, route_gates, out_grad, w_gate, w_up, w_down):
    experts = w_gate.shape[0] * lax.axis_size("expert")
    toks, fan_out = routes.shape
    dim = tokens.shape[1]
    hid = w_gate.shape[2]
    cap = 3 * toks * fan_out // (2 * experts)
    slots = experts * cap
    main = CHUNKS * dim // (CHUNKS + 1)
    packed = experts * ROWS
    DMA = pltpu.SemaphoreType.DMA
    routes_t = routes.T
    gates_t = route_gates.T
    share = dim // lax.axis_size("dp")
    send, mine = call(
        functools.partial(dispatch_kernel, experts, cap),
        (VMEM, VMEM, HBM, HBM, HBM, HBM, HBM),
        [((2 * packed, main), BF, HBM), ((share, 3 * hid), BF, HBM)],
        [
            pltpu.VMEM((toks, dim), BF), pltpu.VMEM((toks, dim), BF), pltpu.VMEM((2 * packed, main), BF),
            pltpu.VMEM(w_down.shape[1:], BF), pltpu.VMEM((share, 3 * hid), BF),
            DMA((2,)), DMA((experts // 16,)), DMA((4,)),
        ],
        limit=63, flops=8 * packed * toks * main, moved=4 * packed * main,
    )(routes_t, gates_t, tokens, out_grad, w_gate[0], w_up[0], w_down[0])
    weights = lax.all_gather(mine, "dp", axis=0, tiled=True)
    recv = lax.all_to_all(
        send.reshape(experts, 2 * ROWS, main), "expert", split_axis=0, concat_axis=0, tiled=True
    ).reshape(2 * packed, main)

    ret, down = call(
        functools.partial(expert_kernel, cap),
        (HBM, HBM),
        [((packed, main + 128), BF, HBM), ((hid, dim), BF, HBM)],
        [
            pltpu.VMEM((2 * packed, main), BF), pltpu.VMEM((dim, 3 * hid), BF), pltpu.VMEM((hid, dim), BF),
            pltpu.VMEM((slots, dim), BF), pltpu.VMEM((slots, dim), BF), pltpu.VMEM((slots, 2 * hid), BF),
            pltpu.VMEM((slots, dim), BF), pltpu.VMEM((packed, main + 128), BF), pltpu.VMEM((hid, dim), BF),
            DMA((1,)), DMA((experts // 16,)), DMA((experts // 16,)), DMA((CHUNKS + 1,)),
        ],
        limit=62, flops=12 * slots * dim * hid, moved=16 * slots * dim,
    )(recv, weights)
    down_grad = lax.psum_scatter(down, "dp", scatter_dimension=0, tiled=True)[None]
    back = lax.all_to_all(
        ret.reshape(experts, ROWS, main + 128), "expert", split_axis=0, concat_axis=0, tiled=True
    ).reshape(packed, main + 128)
    (after,) = call(
        after_kernel, (HBM,), [((8, 128), F32, VMEM)], flops=10**11, moved=10**9,
    )(down_grad[0])
    token_grad, gate_grad = call(
        functools.partial(combine_kernel, experts, cap), (VMEM, VMEM, VMEM, VMEM),
        [((toks, dim), BF, VMEM), ((fan_out, toks), BF, VMEM)],
        limit=16, flops=4 * toks * packed * dim, moved=4 * packed * dim,
    )(routes_t, gates_t, back, after)
    return token_grad, gate_grad.T, down_grad


def solution(mesh):
    rows = P(("dp", "expert"), None)
    weights = P("expert", "dp", None)
    return jax.shard_map(
        local,
        mesh=mesh,
        in_specs=(rows, rows, rows, rows, weights, weights, weights),
        out_specs=(rows, rows, weights),
        check_vma=False,
    )
```

```python
import functools

import jax
import jax.numpy as jnp
from jax import lax
from jax.experimental import pallas as pl
from jax.experimental.pallas import tpu as pltpu
from jax.sharding import PartitionSpec as P

BF = jnp.bfloat16
F32 = jnp.float32
NT = (((1,), (1,)), ((), ()))
TN = (((0,), (0,)), ((), ()))


def iota(shape, axis):
    return lax.broadcasted_iota(jnp.int32, shape, axis)


def slot_keys(routes_ref, experts):
    toks = routes_ref.shape[1]
    rows = iota((experts, toks), 0)
    first = routes_ref[0:1, :] == rows
    second = routes_ref[1:2, :] == rows
    named = jnp.where(first, 1.0, jnp.where(second, 1.0, 0.0))
    earlier = jnp.where(iota((toks, toks), 0) < iota((toks, toks), 1), 1.0, 0.0).astype(BF)
    before = jnp.dot(named.astype(BF), earlier, preferred_element_type=F32)
    return jnp.where(named > 0.5, before, -1.0), first, second


ROWS = 8
CHUNKS = 3


def tail_slot(p, q, cap):
    return (p - cap) * CHUNKS + q


def dispatch_kernel(
    experts, cap, routes_ref, gates_ref, tokens_ref, grads_ref, gate_hbm, up_hbm, down_hbm, send_ref, weights_hbm,
    tok_ref, grad_ref, out_ref, down_ref, pack_ref, in_sems, out_sems, weight_sems,
):
    toks, dim = tokens_ref.shape
    wide = dim // (CHUNKS + 1)
    hid = gate_hbm.shape[1]
    load_down = pltpu.make_async_copy(down_hbm, down_ref, weight_sems.at[3])
    load_down.start()
    load_slices = []
    for i, src in enumerate((gate_hbm, up_hbm)):
        load_slices.append(pltpu.make_async_copy(src, pack_ref.at[:, pl.ds(i * hid, hid)], weight_sems.at[i]))
        load_slices[-1].start()
    loads = []
    for a, (src, dst) in enumerate(((tokens_ref, tok_ref), (grads_ref, grad_ref))):
        loads.append(pltpu.make_async_copy(src, dst, in_sems.at[a]))
        loads[-1].start()
    keys, first, second = slot_keys(routes_ref, experts)
    gates = gates_ref[...].astype(F32)
    gate = jnp.where(first, gates[0:1, :], jnp.where(second, gates[1:2, :], 0.0))
    block = 16
    size = block * ROWS
    p = iota((block, ROWS, toks), 1)
    main_slot = jnp.where(p < cap, p, -2).astype(F32)
    tail_slots = [jnp.where(p < cap, -2, tail_slot(p, q, cap)).astype(F32) for q in range(CHUNKS)]
    load_down.wait()
    for r in range(down_ref.shape[0] // 16):
        for l in range(dim // 128):
            pack_ref[l * 16:(l + 1) * 16, 2 * hid + r * 128:2 * hid + (r + 1) * 128] = (
                down_ref[r * 16:(r + 1) * 16, l * 128:(l + 1) * 128]
            )
    for load in load_slices:
        load.wait()
    stores = [pltpu.make_async_copy(pack_ref, weights_hbm, weight_sems.at[2])]
    stores[0].start()
    for load in loads:
        load.wait()
    for b in range(experts // block):
        key = keys[b * block:(b + 1) * block][:, None, :]
        g = gate[b * block:(b + 1) * block][:, None, :]
        hits = [jnp.where(key == slot, 1.0, 0.0) for slot in [main_slot] + tail_slots]
        plain = [hit.reshape(size, toks).astype(BF) for hit in hits]
        gated = [(hit * g).reshape(size, toks).astype(BF) for hit in hits]
        at = pl.ds(b * 2 * size, 2 * size)
        for q in range(CHUNKS):
            cols = slice(q * wide, (q + 1) * wide)
            both = []
            for ref, placing in ((tok_ref, plain), (grad_ref, gated)):
                lhs = jnp.concatenate([placing[0], placing[1 + q]], axis=1)
                rhs = jnp.concatenate([ref[:, cols], ref[:, CHUNKS * wide:]], axis=0)
                both.append(jnp.dot(lhs, rhs, preferred_element_type=F32).reshape(block, ROWS, wide))
            out_ref[b * 2 * size:(b + 1) * 2 * size, cols] = (
                jnp.concatenate(both, axis=1).reshape(2 * size, wide).astype(BF)
            )
        stores.append(pltpu.make_async_copy(out_ref.at[at, :], send_ref.at[at, :], out_sems.at[b]))
        stores[-1].start()
    for store in stores:
        store.wait()


def expert_kernel(
    cap, recv_hbm, wgu_hbm, ret_hbm, down_hbm,
    recv_ref, wgu_ref, wd_ref, x_ref, scaled_ref, ggu_ref, part_ref, ret_ref, down_ref,
    in_sems, recv_sems, out_sems, down_sems,
):
    hid, dim = wd_ref.shape
    wide = dim // (CHUNKS + 1)
    tail = CHUNKS * wide
    block = 16
    size = 2 * block * ROWS
    count = block * cap
    blocks = recv_ref.shape[0] // size
    loads = []
    for b in range(blocks):
        at = pl.ds(b * size, size)
        loads.append(pltpu.make_async_copy(recv_hbm.at[at, :], recv_ref.at[at, :], recv_sems.at[b]))
        loads[-1].start()
    lanes = [pl.ds(2 * hid, hid), pl.ds(0, 2 * hid)]
    load_down, load_wgu = (
        pltpu.make_async_copy(wgu_hbm.at[:, at], wgu_ref.at[:, at], in_sems.at[i]) for i, at in enumerate(lanes)
    )
    load_down.start()
    load_wgu.start()
    few = 2 * block

    def unpack(a, q):
        height = count if q is None else few
        out_row = iota((height, 1), 0)
        source, half = out_row % block, out_row // block % 2
        row = half * CHUNKS + out_row // few if q is None else cap + half
        return jnp.where(source * (2 * ROWS) + a * ROWS + row == iota((height, size), 1), 1.0, 0.0).astype(BF)

    mains = [unpack(0, None), unpack(1, None)]
    perm = jnp.concatenate(mains + [unpack(0, 0), unpack(1, 0)], axis=0)
    for b in range(blocks):
        loads[b].wait()
        at = slice(b * count, (b + 1) * count)
        for q in range(CHUNKS):
            cols = slice(q * wide, (q + 1) * wide)
            tails = slice(b * count + q * few, b * count + (q + 1) * few)
            moved = jnp.dot(
                perm, recv_ref[b * size:(b + 1) * size, cols], preferred_element_type=F32
            ).astype(BF)
            x_ref[at, cols] = moved[:count]
            scaled_ref[at, cols] = moved[count:2 * count]
            x_ref[tails, tail:] = moved[2 * count:2 * count + few]
            scaled_ref[tails, tail:] = moved[2 * count + few:]
    load_down.wait()
    unpack_down(wgu_ref, wd_ref)
    hidden_grad = lax.dot_general(scaled_ref[...], wd_ref[...], NT, preferred_element_type=F32)
    load_wgu.wait()
    pre_gate = jnp.dot(x_ref[...], wgu_ref[:, :hid], preferred_element_type=F32)
    pre_up = jnp.dot(x_ref[...], wgu_ref[:, hid:2 * hid], preferred_element_type=F32)
    squash = jax.nn.sigmoid(pre_gate)
    activated = pre_gate * squash
    hidden = (activated * pre_up).astype(BF)
    ggu_ref[:, :hid] = (hidden_grad * pre_up * squash * (1.0 + pre_gate * (1.0 - squash))).astype(BF)
    ggu_ref[:, hid:] = (hidden_grad * activated).astype(BF)
    dots = jnp.sum(hidden.astype(F32) * hidden_grad, axis=1, keepdims=True)
    high = dots.astype(BF).astype(F32)
    lane = iota((dots.shape[0], 128), 1)
    pair = jnp.where(lane == 0, high, jnp.where(lane == 1, dots - high, 0.0)).astype(BF)
    stores = []
    for q in range(CHUNKS + 1):
        at = slice(q * wide, (q + 1) * wide)
        part_ref[:, at] = lax.dot_general(
            ggu_ref[...], wgu_ref[at, :2 * hid], NT, preferred_element_type=F32
        ).astype(BF)
    size = 2 * block * ROWS
    out_row = iota((size, 1), 0)
    which, source, p = out_row // (block * ROWS), out_row // ROWS % block, out_row % ROWS
    slot_row = which * count + (p % CHUNKS) * few + p // CHUNKS * block + source
    tail_row = 2 * count + which * few + (p - cap) * block + source
    width = 2 * (count + few)
    perm = jnp.where(jnp.where(p < cap, slot_row, tail_row) == iota((size, width), 1), 1.0, 0.0).astype(BF)
    for b in range(blocks // 2):
        first = 2 * b * count
        at = slice(first, first + 2 * count)
        out = slice(b * size, (b + 1) * size)
        for q in range(CHUNKS):
            cols = slice(q * wide, (q + 1) * wide)
            pieces = [part_ref[at, cols]]
            for start in (first + q * few, first + count + q * few):
                pieces.append(part_ref[start:start + few, tail:])
            rhs = jnp.concatenate(pieces, axis=0)
            ret_ref[out, cols] = jnp.dot(perm, rhs, preferred_element_type=F32).astype(BF)
        ret_ref[out, tail:] = jnp.dot(perm[:, :2 * count], pair[at], preferred_element_type=F32).astype(BF)
        rows = pl.ds(b * size, size)
        stores.append(pltpu.make_async_copy(ret_ref.at[rows, :], ret_hbm.at[rows, :], out_sems.at[b]))
        stores[-1].start()
    for q in range(CHUNKS + 1):
        cols = pl.ds(q * wide, wide)
        at = slice(q * wide, (q + 1) * wide)
        down_ref[:, at] = lax.dot_general(hidden, scaled_ref[:, at], TN, preferred_element_type=F32).astype(BF)
        stores.append(pltpu.make_async_copy(down_ref.at[:, cols], down_hbm.at[:, cols], down_sems.at[q]))
        stores[-1].start()
    for store in stores:
        store.wait()


def unpack_down(packed_ref, down_ref):
    hid, dim = down_ref.shape
    lanes = packed_ref.shape[1] - hid
    high = 16 * (dim // 128)
    each = hid * high // packed_ref.shape[0]
    for part in range(packed_ref.shape[0] // high):
        for r in range(each // 16):
            for l in range(dim // 128):
                down_ref[part * each + r * 16:part * each + (r + 1) * 16, l * 128:(l + 1) * 128] = packed_ref[
                    part * high + l * 16:part * high + (l + 1) * 16, lanes + r * 128:lanes + (r + 1) * 128
                ]


def combine_kernel(experts, cap, routes_ref, gates_ref, back_ref, after_ref, token_grad_ref, gate_grad_ref):
    toks, dim = token_grad_ref.shape
    wide = dim // (CHUNKS + 1)
    tail = CHUNKS * wide
    packed = experts * ROWS
    keys, first, _ = slot_keys(routes_ref, experts)
    spread = jnp.where(iota((experts, packed), 0) == iota((experts, packed), 1) // ROWS, 1.0, 0.0).astype(BF)
    key = lax.dot_general(keys.astype(BF), spread, TN, preferred_element_type=F32)
    one = lax.dot_general(jnp.where(first, 1.0, 0.0).astype(BF), spread, TN, preferred_element_type=F32)
    p = iota((1, packed), 1) % ROWS
    main_slot = jnp.where(p < cap, p, -2).astype(F32)
    main = jnp.where(key == main_slot, 1.0, 0.0)
    choices = jnp.concatenate([main * one, main * (1.0 - one)], axis=0).astype(BF)
    lhs = []
    for q in range(CHUNKS):
        slot = jnp.where(p < cap, -2, tail_slot(p, q, cap)).astype(F32)
        lhs.append(jnp.concatenate([main, jnp.where(key == slot, 1.0, 0.0)], axis=0).astype(BF))
    tails = None
    for q in range(CHUNKS):
        cols = slice(q * wide, (q + 1) * wide)
        moved = jnp.dot(lhs[q], back_ref[:, cols], preferred_element_type=F32)
        token_grad_ref[:, cols] = moved[:toks].astype(BF)
        tails = moved[toks:] if tails is None else tails + moved[toks:]
    token_grad_ref[:, tail:] = tails.astype(BF)
    dots = jnp.dot(choices, back_ref[:, tail:], preferred_element_type=F32)
    gates = gates_ref[...].astype(F32)
    rows = []
    for k in range(2):
        pair = dots[k * toks:(k + 1) * toks].T
        rows.append((pair[0:1] + pair[1:2]) / gates[k:k + 1])
    gate_grad_ref[...] = jnp.concatenate(rows, axis=0).astype(BF)


def after_kernel(down_ref, out_ref):
    out_ref[...] = jnp.zeros_like(out_ref)


VMEM = pl.BlockSpec(memory_space=pltpu.VMEM)
SMEM = pl.BlockSpec(memory_space=pltpu.SMEM)
HBM = pl.BlockSpec(memory_space=pltpu.HBM)


def call(kernel, ins, outs, scratch=(), limit=16, flops=0, moved=0):
    return pl.pallas_call(
        kernel,
        out_shape=tuple(jax.ShapeDtypeStruct(shape, kind) for shape, kind, _ in outs),
        in_specs=list(ins),
        out_specs=tuple(spec for _, _, spec in outs),
        scratch_shapes=list(scratch),
        compiler_params=pltpu.CompilerParams(vmem_limit_bytes=limit * 1024 * 1024),
        cost_estimate=pl.CostEstimate(flops=flops, bytes_accessed=moved, transcendentals=0),
    )


def local(tokens, routes, route_gates, out_grad, w_gate, w_up, w_down):
    experts = w_gate.shape[0] * lax.axis_size("expert")
    toks, fan_out = routes.shape
    dim = tokens.shape[1]
    hid = w_gate.shape[2]
    cap = 3 * toks * fan_out // (2 * experts)
    slots = experts * cap
    main = CHUNKS * dim // (CHUNKS + 1)
    packed = experts * ROWS
    DMA = pltpu.SemaphoreType.DMA
    routes_t = routes.T
    gates_t = route_gates.T
    share = dim // lax.axis_size("dp")
    send, mine = call(
        functools.partial(dispatch_kernel, experts, cap),
        (VMEM, VMEM, HBM, HBM, HBM, HBM, HBM),
        [((2 * packed, main), BF, HBM), ((share, 3 * hid), BF, HBM)],
        [
            pltpu.VMEM((toks, dim), BF), pltpu.VMEM((toks, dim), BF), pltpu.VMEM((2 * packed, main), BF),
            pltpu.VMEM(w_down.shape[1:], BF), pltpu.VMEM((share, 3 * hid), BF),
            DMA((2,)), DMA((experts // 16,)), DMA((4,)),
        ],
        limit=63, flops=8 * packed * toks * main, moved=4 * packed * main,
    )(routes_t, gates_t, tokens, out_grad, w_gate[0], w_up[0], w_down[0])
    weights = lax.all_gather(mine, "dp", axis=0, tiled=True)
    recv = lax.all_to_all(
        send.reshape(experts, 2 * ROWS, main), "expert", split_axis=0, concat_axis=0, tiled=True
    ).reshape(2 * packed, main)

    ret, down = call(
        functools.partial(expert_kernel, cap),
        (HBM, HBM),
        [((packed, main + 128), BF, HBM), ((hid, dim), BF, HBM)],
        [
            pltpu.VMEM((2 * packed, main), BF), pltpu.VMEM((dim, 3 * hid), BF), pltpu.VMEM((hid, dim), BF),
            pltpu.VMEM((slots, dim), BF), pltpu.VMEM((slots, dim), BF), pltpu.VMEM((slots, 2 * hid), BF),
            pltpu.VMEM((slots, dim), BF), pltpu.VMEM((packed, main + 128), BF), pltpu.VMEM((hid, dim), BF),
            DMA((2,)), DMA((experts // 16,)), DMA((experts // 32,)), DMA((CHUNKS + 1,)),
        ],
        limit=62, flops=12 * slots * dim * hid, moved=16 * slots * dim,
    )(recv, weights)
    down_grad = lax.psum_scatter(down, "dp", scatter_dimension=0, tiled=True)[None]
    back = lax.all_to_all(
        ret.reshape(experts, ROWS, main + 128), "expert", split_axis=0, concat_axis=0, tiled=True
    ).reshape(packed, main + 128)
    (after,) = call(
        after_kernel, (HBM,), [((8, 128), F32, VMEM)], flops=10**11, moved=10**9,
    )(down_grad[0])
    token_grad, gate_grad = call(
        functools.partial(combine_kernel, experts, cap), (VMEM, VMEM, VMEM, VMEM),
        [((toks, dim), BF, VMEM), ((fan_out, toks), BF, VMEM)],
        limit=16, flops=4 * toks * packed * dim, moved=4 * packed * dim,
    )(routes_t, gates_t, back, after)
    return token_grad, gate_grad.T, down_grad


def solution(mesh):
    rows = P(("dp", "expert"), None)
    weights = P("expert", "dp", None)
    return jax.shard_map(
        local,
        mesh=mesh,
        in_specs=(rows, rows, rows, rows, weights, weights, weights),
        out_specs=(rows, rows, weights),
        check_vma=False,
    )
```

```python
import functools

import jax
import jax.numpy as jnp
from jax import lax
from jax.experimental import pallas as pl
from jax.experimental.pallas import tpu as pltpu
from jax.sharding import PartitionSpec as P

BF = jnp.bfloat16
F32 = jnp.float32
NT = (((1,), (1,)), ((), ()))
TN = (((0,), (0,)), ((), ()))


def iota(shape, axis):
    return lax.broadcasted_iota(jnp.int32, shape, axis)


def slot_keys(routes_ref, experts):
    toks = routes_ref.shape[1]
    rows = iota((experts, toks), 0)
    first = routes_ref[0:1, :] == rows
    second = routes_ref[1:2, :] == rows
    named = jnp.where(first, 1.0, jnp.where(second, 1.0, 0.0))
    earlier = jnp.where(iota((toks, toks), 0) < iota((toks, toks), 1), 1.0, 0.0).astype(BF)
    before = jnp.dot(named.astype(BF), earlier, preferred_element_type=F32)
    return jnp.where(named > 0.5, before, -1.0), first, second


ROWS = 8
CHUNKS = 3


def tail_slot(p, q, cap):
    return (p - cap) * CHUNKS + q


def dispatch_kernel(
    experts, cap, routes_ref, gates_ref, tokens_ref, grads_ref, gate_hbm, up_hbm, down_hbm, send_ref, weights_hbm,
    tok_ref, grad_ref, out_ref, down_ref, pack_ref, in_sems, out_sems, weight_sems,
):
    toks, dim = tokens_ref.shape
    wide = dim // (CHUNKS + 1)
    hid = gate_hbm.shape[1]
    load_down = pltpu.make_async_copy(down_hbm, down_ref, weight_sems.at[3])
    load_down.start()
    load_slices = []
    for i, src in enumerate((gate_hbm, up_hbm)):
        load_slices.append(pltpu.make_async_copy(src, pack_ref.at[:, pl.ds(i * hid, hid)], weight_sems.at[i]))
        load_slices[-1].start()
    loads = []
    for a, (src, dst) in enumerate(((tokens_ref, tok_ref), (grads_ref, grad_ref))):
        loads.append(pltpu.make_async_copy(src, dst, in_sems.at[a]))
        loads[-1].start()
    keys, first, second = slot_keys(routes_ref, experts)
    gates = gates_ref[...].astype(F32)
    gate = jnp.where(first, gates[0:1, :], jnp.where(second, gates[1:2, :], 0.0))
    block = 16
    size = block * ROWS
    p = iota((block, ROWS, toks), 1)
    main_slot = jnp.where(p < cap, p, -2).astype(F32)
    tail_slots = [jnp.where(p < cap, -2, tail_slot(p, q, cap)).astype(F32) for q in range(CHUNKS)]
    load_down.wait()
    for r in range(down_ref.shape[0] // 16):
        for l in range(dim // 128):
            pack_ref[l * 16:(l + 1) * 16, 2 * hid + r * 128:2 * hid + (r + 1) * 128] = (
                down_ref[r * 16:(r + 1) * 16, l * 128:(l + 1) * 128]
            )
    for load in load_slices:
        load.wait()
    stores = [pltpu.make_async_copy(pack_ref, weights_hbm, weight_sems.at[2])]
    stores[0].start()
    for load in loads:
        load.wait()
    for b in range(experts // block):
        key = keys[b * block:(b + 1) * block][:, None, :]
        g = gate[b * block:(b + 1) * block][:, None, :]
        hits = [jnp.where(key == slot, 1.0, 0.0) for slot in [main_slot] + tail_slots]
        plain = [hit.reshape(size, toks).astype(BF) for hit in hits]
        gated = [(hit * g).reshape(size, toks).astype(BF) for hit in hits]
        at = pl.ds(b * 2 * size, 2 * size)
        for q in range(CHUNKS):
            cols = slice(q * wide, (q + 1) * wide)
            both = []
            for ref, placing in ((tok_ref, plain), (grad_ref, gated)):
                lhs = jnp.concatenate([placing[0], placing[1 + q]], axis=1)
                rhs = jnp.concatenate([ref[:, cols], ref[:, CHUNKS * wide:]], axis=0)
                both.append(jnp.dot(lhs, rhs, preferred_element_type=F32).reshape(block, ROWS, wide))
            out_ref[b * 2 * size:(b + 1) * 2 * size, cols] = (
                jnp.concatenate(both, axis=1).reshape(2 * size, wide).astype(BF)
            )
        stores.append(pltpu.make_async_copy(out_ref.at[at, :], send_ref.at[at, :], out_sems.at[b]))
        stores[-1].start()
    for store in stores:
        store.wait()


def expert_kernel(
    cap, recv_hbm, wgu_hbm, ret_hbm, down_hbm,
    recv_ref, wgu_ref, wd_ref, x_ref, scaled_ref, ggu_ref, part_ref, ret_ref, down_ref,
    in_sems, recv_sems, out_sems, down_sems,
):
    hid, dim = wd_ref.shape
    wide = dim // (CHUNKS + 1)
    tail = CHUNKS * wide
    block = 16
    size = 2 * block * ROWS
    count = block * cap
    blocks = recv_ref.shape[0] // size
    loads = []
    for b in range(blocks):
        at = pl.ds(b * size, size)
        loads.append(pltpu.make_async_copy(recv_hbm.at[at, :], recv_ref.at[at, :], recv_sems.at[b]))
        loads[-1].start()
    lanes = [pl.ds(2 * hid, hid), pl.ds(0, 2 * hid)]
    load_down, load_wgu = (
        pltpu.make_async_copy(wgu_hbm.at[:, at], wgu_ref.at[:, at], in_sems.at[i]) for i, at in enumerate(lanes)
    )
    load_down.start()
    load_wgu.start()
    few = 2 * block

    def unpack(a, q):
        height = count if q is None else few
        out_row = iota((height, 1), 0)
        source, half = out_row % block, out_row // block % 2
        row = half * CHUNKS + out_row // few if q is None else cap + half
        return jnp.where(source * (2 * ROWS) + a * ROWS + row == iota((height, size), 1), 1.0, 0.0).astype(BF)

    mains = [unpack(0, None), unpack(1, None)]
    perm = jnp.concatenate(mains + [unpack(0, 0), unpack(1, 0)], axis=0)
    for b in range(blocks):
        loads[b].wait()
        at = slice(b * count, (b + 1) * count)
        for q in range(CHUNKS):
            cols = slice(q * wide, (q + 1) * wide)
            tails = slice(b * count + q * few, b * count + (q + 1) * few)
            moved = jnp.dot(
                perm, recv_ref[b * size:(b + 1) * size, cols], preferred_element_type=F32
            ).astype(BF)
            x_ref[at, cols] = moved[:count]
            scaled_ref[at, cols] = moved[count:2 * count]
            x_ref[tails, tail:] = moved[2 * count:2 * count + few]
            scaled_ref[tails, tail:] = moved[2 * count + few:]
    load_down.wait()
    unpack_down(wgu_ref, wd_ref)
    hidden_grad = lax.dot_general(scaled_ref[...], wd_ref[...], NT, preferred_element_type=F32)
    load_wgu.wait()
    pre_gate = jnp.dot(x_ref[...], wgu_ref[:, :hid], preferred_element_type=F32)
    pre_up = jnp.dot(x_ref[...], wgu_ref[:, hid:2 * hid], preferred_element_type=F32)
    squash = jax.nn.sigmoid(pre_gate)
    activated = pre_gate * squash
    hidden = (activated * pre_up).astype(BF)
    ggu_ref[:, :hid] = (hidden_grad * pre_up * squash * (1.0 + pre_gate * (1.0 - squash))).astype(BF)
    ggu_ref[:, hid:] = (hidden_grad * activated).astype(BF)
    dots = jnp.sum(hidden.astype(F32) * hidden_grad, axis=1, keepdims=True)
    high = dots.astype(BF).astype(F32)
    lane = iota((dots.shape[0], 128), 1)
    pair = jnp.where(lane == 0, high, jnp.where(lane == 1, dots - high, 0.0)).astype(BF)
    stores = []
    for q in range(CHUNKS + 1):
        at = slice(q * wide, (q + 1) * wide)
        part_ref[:, at] = lax.dot_general(
            ggu_ref[...], wgu_ref[at, :2 * hid], NT, preferred_element_type=F32
        ).astype(BF)
    size = 2 * block * ROWS
    out_row = iota((size, 1), 0)
    which, source, p = out_row // (block * ROWS), out_row // ROWS % block, out_row % ROWS
    slot_row = which * count + (p % CHUNKS) * few + p // CHUNKS * block + source
    tail_row = 2 * count + which * few + (p - cap) * block + source
    width = 2 * (count + few)
    perm = jnp.where(jnp.where(p < cap, slot_row, tail_row) == iota((size, width), 1), 1.0, 0.0).astype(BF)
    for b in range(blocks // 2):
        first = 2 * b * count
        at = slice(first, first + 2 * count)
        out = slice(b * size, (b + 1) * size)
        for q in range(CHUNKS):
            cols = slice(q * wide, (q + 1) * wide)
            pieces = [part_ref[at, cols]]
            for start in (first + q * few, first + count + q * few):
                pieces.append(part_ref[start:start + few, tail:])
            rhs = jnp.concatenate(pieces, axis=0)
            ret_ref[out, cols] = jnp.dot(perm, rhs, preferred_element_type=F32).astype(BF)
        ret_ref[out, tail:] = jnp.dot(perm[:, :2 * count], pair[at], preferred_element_type=F32).astype(BF)
        rows = pl.ds(b * size, size)
        stores.append(pltpu.make_async_copy(ret_ref.at[rows, :], ret_hbm.at[rows, :], out_sems.at[b]))
        stores[-1].start()
    for q in range(CHUNKS + 1):
        cols = pl.ds(q * wide, wide)
        at = slice(q * wide, (q + 1) * wide)
        down_ref[:, at] = lax.dot_general(hidden, scaled_ref[:, at], TN, preferred_element_type=F32).astype(BF)
        stores.append(pltpu.make_async_copy(down_ref.at[:, cols], down_hbm.at[:, cols], down_sems.at[q]))
        stores[-1].start()
    for store in stores:
        store.wait()


def unpack_down(packed_ref, down_ref):
    hid, dim = down_ref.shape
    lanes = packed_ref.shape[1] - hid
    high = 16 * (dim // 128)
    each = hid * high // packed_ref.shape[0]
    for part in range(packed_ref.shape[0] // high):
        for r in range(each // 16):
            for l in range(dim // 128):
                down_ref[part * each + r * 16:part * each + (r + 1) * 16, l * 128:(l + 1) * 128] = packed_ref[
                    part * high + l * 16:part * high + (l + 1) * 16, lanes + r * 128:lanes + (r + 1) * 128
                ]


def combine_kernel(gates_ref, back_ref, hot_ref, token_grad_ref, gate_grad_ref):
    toks, dim = token_grad_ref.shape
    wide = dim // (CHUNKS + 1)
    tail = CHUNKS * wide
    tails = None
    for q in range(CHUNKS):
        cols = slice(q * wide, (q + 1) * wide)
        moved = jnp.dot(hot_ref[q * 2 * toks:(q + 1) * 2 * toks, :], back_ref[:, cols], preferred_element_type=F32)
        token_grad_ref[:, cols] = moved[:toks].astype(BF)
        tails = moved[toks:] if tails is None else tails + moved[toks:]
    token_grad_ref[:, tail:] = tails.astype(BF)
    dots = jnp.dot(hot_ref[CHUNKS * 2 * toks:, :], back_ref[:, tail:], preferred_element_type=F32)
    gates = gates_ref[...].astype(F32)
    rows = []
    for k in range(2):
        pair = dots[k * toks:(k + 1) * toks].T
        rows.append((pair[0:1] + pair[1:2]) / gates[k:k + 1])
    gate_grad_ref[...] = jnp.concatenate(rows, axis=0).astype(BF)


def hot_kernel(experts, cap, routes_ref, after_ref, hot_ref):
    toks = routes_ref.shape[1]
    packed = experts * ROWS
    keys, first, _ = slot_keys(routes_ref, experts)
    spread = jnp.where(iota((experts, packed), 0) == iota((experts, packed), 1) // ROWS, 1.0, 0.0).astype(BF)
    key = lax.dot_general(keys.astype(BF), spread, TN, preferred_element_type=F32)
    one = lax.dot_general(jnp.where(first, 1.0, 0.0).astype(BF), spread, TN, preferred_element_type=F32)
    p = iota((1, packed), 1) % ROWS
    main_slot = jnp.where(p < cap, p, -2).astype(F32)
    main = jnp.where(key == main_slot, 1.0, 0.0)
    hot_ref[CHUNKS * 2 * toks:, :] = jnp.concatenate([main * one, main * (1.0 - one)], axis=0).astype(BF)
    for q in range(CHUNKS):
        slot = jnp.where(p < cap, -2, tail_slot(p, q, cap)).astype(F32)
        hot_ref[q * 2 * toks:(q + 1) * 2 * toks, :] = (
            jnp.concatenate([main, jnp.where(key == slot, 1.0, 0.0)], axis=0).astype(BF)
        )


VMEM = pl.BlockSpec(memory_space=pltpu.VMEM)
SMEM = pl.BlockSpec(memory_space=pltpu.SMEM)
HBM = pl.BlockSpec(memory_space=pltpu.HBM)


def call(kernel, ins, outs, scratch=(), limit=16, flops=0, moved=0):
    return pl.pallas_call(
        kernel,
        out_shape=tuple(jax.ShapeDtypeStruct(shape, kind) for shape, kind, _ in outs),
        in_specs=list(ins),
        out_specs=tuple(spec for _, _, spec in outs),
        scratch_shapes=list(scratch),
        compiler_params=pltpu.CompilerParams(vmem_limit_bytes=limit * 1024 * 1024),
        cost_estimate=pl.CostEstimate(flops=flops, bytes_accessed=moved, transcendentals=0),
    )


def local(tokens, routes, route_gates, out_grad, w_gate, w_up, w_down):
    experts = w_gate.shape[0] * lax.axis_size("expert")
    toks, fan_out = routes.shape
    dim = tokens.shape[1]
    hid = w_gate.shape[2]
    cap = 3 * toks * fan_out // (2 * experts)
    slots = experts * cap
    main = CHUNKS * dim // (CHUNKS + 1)
    packed = experts * ROWS
    DMA = pltpu.SemaphoreType.DMA
    routes_t = routes.T
    gates_t = route_gates.T
    share = dim // lax.axis_size("dp")
    send, mine = call(
        functools.partial(dispatch_kernel, experts, cap),
        (VMEM, VMEM, HBM, HBM, HBM, HBM, HBM),
        [((2 * packed, main), BF, HBM), ((share, 3 * hid), BF, HBM)],
        [
            pltpu.VMEM((toks, dim), BF), pltpu.VMEM((toks, dim), BF), pltpu.VMEM((2 * packed, main), BF),
            pltpu.VMEM(w_down.shape[1:], BF), pltpu.VMEM((share, 3 * hid), BF),
            DMA((2,)), DMA((experts // 16,)), DMA((4,)),
        ],
        limit=63, flops=8 * packed * toks * main, moved=4 * packed * main,
    )(routes_t, gates_t, tokens, out_grad, w_gate[0], w_up[0], w_down[0])
    weights = lax.all_gather(mine, "dp", axis=0, tiled=True)
    recv = lax.all_to_all(
        send.reshape(experts, 2 * ROWS, main), "expert", split_axis=0, concat_axis=0, tiled=True
    ).reshape(2 * packed, main)

    ret, down = call(
        functools.partial(expert_kernel, cap),
        (HBM, HBM),
        [((packed, main + 128), BF, HBM), ((hid, dim), BF, HBM)],
        [
            pltpu.VMEM((2 * packed, main), BF), pltpu.VMEM((dim, 3 * hid), BF), pltpu.VMEM((hid, dim), BF),
            pltpu.VMEM((slots, dim), BF), pltpu.VMEM((slots, dim), BF), pltpu.VMEM((slots, 2 * hid), BF),
            pltpu.VMEM((slots, dim), BF), pltpu.VMEM((packed, main + 128), BF), pltpu.VMEM((hid, dim), BF),
            DMA((2,)), DMA((experts // 16,)), DMA((experts // 32,)), DMA((CHUNKS + 1,)),
        ],
        limit=62, flops=12 * slots * dim * hid, moved=16 * slots * dim,
    )(recv, weights)
    down_grad = lax.psum_scatter(down, "dp", scatter_dimension=0, tiled=True)[None]
    back = lax.all_to_all(
        ret.reshape(experts, ROWS, main + 128), "expert", split_axis=0, concat_axis=0, tiled=True
    ).reshape(packed, main + 128)
    (hot,) = call(
        functools.partial(hot_kernel, experts, cap), (VMEM, HBM),
        [((2 * (CHUNKS + 1) * toks, packed), BF, VMEM)], flops=10**11, moved=10**9,
    )(routes_t, down_grad[0])
    token_grad, gate_grad = call(
        combine_kernel, (VMEM, VMEM, VMEM),
        [((toks, dim), BF, VMEM), ((fan_out, toks), BF, VMEM)],
        limit=16, flops=4 * toks * packed * dim, moved=4 * packed * dim,
    )(gates_t, back, hot)
    return token_grad, gate_grad.T, down_grad


def solution(mesh):
    rows = P(("dp", "expert"), None)
    weights = P("expert", "dp", None)
    return jax.shard_map(
        local,
        mesh=mesh,
        in_specs=(rows, rows, rows, rows, weights, weights, weights),
        out_specs=(rows, rows, weights),
        check_vma=False,
    )
```

```python
import functools

import jax
import jax.numpy as jnp
from jax import lax
from jax.experimental import pallas as pl
from jax.experimental.pallas import tpu as pltpu
from jax.sharding import PartitionSpec as P

BF = jnp.bfloat16
F32 = jnp.float32
NT = (((1,), (1,)), ((), ()))
TN = (((0,), (0,)), ((), ()))


def iota(shape, axis):
    return lax.broadcasted_iota(jnp.int32, shape, axis)


def slot_keys(routes_ref, experts):
    toks = routes_ref.shape[1]
    rows = iota((experts, toks), 0)
    first = routes_ref[0:1, :] == rows
    second = routes_ref[1:2, :] == rows
    named = jnp.where(first, 1.0, jnp.where(second, 1.0, 0.0))
    earlier = jnp.where(iota((toks, toks), 0) < iota((toks, toks), 1), 1.0, 0.0).astype(BF)
    before = jnp.dot(named.astype(BF), earlier, preferred_element_type=F32)
    return jnp.where(named > 0.5, before, -1.0), first, second


ROWS = 8
CHUNKS = 3


def tail_slot(p, q, cap):
    return (p - cap) * CHUNKS + q


def dispatch_kernel(
    experts, cap, routes_ref, gates_ref, tokens_ref, grads_ref, gate_hbm, up_hbm, down_hbm, send_ref, weights_hbm,
    tok_ref, grad_ref, out_ref, down_ref, pack_ref, in_sems, out_sems, weight_sems,
):
    toks, dim = tokens_ref.shape
    wide = dim // (CHUNKS + 1)
    hid = gate_hbm.shape[1]
    loads = []
    for a, (src, dst) in enumerate(((tokens_ref, tok_ref), (grads_ref, grad_ref))):
        loads.append(pltpu.make_async_copy(src, dst, in_sems.at[a]))
        loads[-1].start()
    load_down = pltpu.make_async_copy(down_hbm, down_ref, weight_sems.at[3])
    load_down.start()
    load_slices = []
    for i, src in enumerate((gate_hbm, up_hbm)):
        load_slices.append(pltpu.make_async_copy(src, pack_ref.at[:, pl.ds(i * hid, hid)], weight_sems.at[i]))
        load_slices[-1].start()
    keys, first, second = slot_keys(routes_ref, experts)
    gates = gates_ref[...].astype(F32)
    gate = jnp.where(first, gates[0:1, :], jnp.where(second, gates[1:2, :], 0.0))
    block = 16
    size = block * ROWS
    p = iota((block, ROWS, toks), 1)
    main_slot = jnp.where(p < cap, p, -2).astype(F32)
    tail_slots = [jnp.where(p < cap, -2, tail_slot(p, q, cap)).astype(F32) for q in range(CHUNKS)]
    stores = []
    for load in loads:
        load.wait()
    for b in range(experts // block):
        key = keys[b * block:(b + 1) * block][:, None, :]
        g = gate[b * block:(b + 1) * block][:, None, :]
        hits = [jnp.where(key == slot, 1.0, 0.0) for slot in [main_slot] + tail_slots]
        plain = [hit.reshape(size, toks).astype(BF) for hit in hits]
        gated = [(hit * g).reshape(size, toks).astype(BF) for hit in hits]
        at = pl.ds(b * 2 * size, 2 * size)
        for q in range(CHUNKS):
            cols = slice(q * wide, (q + 1) * wide)
            both = []
            for ref, placing in ((tok_ref, plain), (grad_ref, gated)):
                lhs = jnp.concatenate([placing[0], placing[1 + q]], axis=1)
                rhs = jnp.concatenate([ref[:, cols], ref[:, CHUNKS * wide:]], axis=0)
                both.append(jnp.dot(lhs, rhs, preferred_element_type=F32).reshape(block, ROWS, wide))
            out_ref[b * 2 * size:(b + 1) * 2 * size, cols] = (
                jnp.concatenate(both, axis=1).reshape(2 * size, wide).astype(BF)
            )
        stores.append(pltpu.make_async_copy(out_ref.at[at, :], send_ref.at[at, :], out_sems.at[b]))
        stores[-1].start()
        if b == 0:
            load_down.wait()
            for r in range(down_ref.shape[0] // 16):
                for l in range(dim // 128):
                    pack_ref[l * 16:(l + 1) * 16, 2 * hid + r * 128:2 * hid + (r + 1) * 128] = (
                        down_ref[r * 16:(r + 1) * 16, l * 128:(l + 1) * 128]
                    )
            for load in load_slices:
                load.wait()
            stores.append(pltpu.make_async_copy(pack_ref, weights_hbm, weight_sems.at[2]))
            stores[-1].start()
    for store in stores:
        store.wait()


def expert_kernel(
    cap, recv_hbm, wgu_hbm, ret_hbm, down_hbm,
    recv_ref, wgu_ref, wd_ref, x_ref, scaled_ref, ggu_ref, part_ref, ret_ref, down_ref,
    in_sems, recv_sems, out_sems, down_sems,
):
    hid, dim = wd_ref.shape
    wide = dim // (CHUNKS + 1)
    tail = CHUNKS * wide
    block = 16
    size = 2 * block * ROWS
    count = block * cap
    blocks = recv_ref.shape[0] // size
    loads = []
    for b in range(blocks):
        at = pl.ds(b * size, size)
        loads.append(pltpu.make_async_copy(recv_hbm.at[at, :], recv_ref.at[at, :], recv_sems.at[b]))
        loads[-1].start()
    lanes = [pl.ds(2 * hid, hid), pl.ds(0, 2 * hid)]
    load_down, load_wgu = (
        pltpu.make_async_copy(wgu_hbm.at[:, at], wgu_ref.at[:, at], in_sems.at[i]) for i, at in enumerate(lanes)
    )
    load_down.start()
    load_wgu.start()
    few = 2 * block

    def unpack(a, q):
        height = count if q is None else few
        out_row = iota((height, 1), 0)
        source, half = out_row % block, out_row // block % 2
        row = half * CHUNKS + out_row // few if q is None else cap + half
        return jnp.where(source * (2 * ROWS) + a * ROWS + row == iota((height, size), 1), 1.0, 0.0).astype(BF)

    mains = [unpack(0, None), unpack(1, None)]
    perm = jnp.concatenate(mains + [unpack(0, 0), unpack(1, 0)], axis=0)
    for b in range(blocks):
        loads[b].wait()
        at = slice(b * count, (b + 1) * count)
        for q in range(CHUNKS):
            cols = slice(q * wide, (q + 1) * wide)
            tails = slice(b * count + q * few, b * count + (q + 1) * few)
            moved = jnp.dot(
                perm, recv_ref[b * size:(b + 1) * size, cols], preferred_element_type=F32
            ).astype(BF)
            x_ref[at, cols] = moved[:count]
            scaled_ref[at, cols] = moved[count:2 * count]
            x_ref[tails, tail:] = moved[2 * count:2 * count + few]
            scaled_ref[tails, tail:] = moved[2 * count + few:]
    load_down.wait()
    unpack_down(wgu_ref, wd_ref)
    hidden_grad = lax.dot_general(scaled_ref[...], wd_ref[...], NT, preferred_element_type=F32)
    load_wgu.wait()
    pre_gate = jnp.dot(x_ref[...], wgu_ref[:, :hid], preferred_element_type=F32)
    pre_up = jnp.dot(x_ref[...], wgu_ref[:, hid:2 * hid], preferred_element_type=F32)
    squash = jax.nn.sigmoid(pre_gate)
    activated = pre_gate * squash
    hidden = (activated * pre_up).astype(BF)
    ggu_ref[:, :hid] = (hidden_grad * pre_up * squash * (1.0 + pre_gate * (1.0 - squash))).astype(BF)
    ggu_ref[:, hid:] = (hidden_grad * activated).astype(BF)
    dots = jnp.sum(hidden.astype(F32) * hidden_grad, axis=1, keepdims=True)
    high = dots.astype(BF).astype(F32)
    lane = iota((dots.shape[0], 128), 1)
    pair = jnp.where(lane == 0, high, jnp.where(lane == 1, dots - high, 0.0)).astype(BF)
    stores = []
    for q in range(CHUNKS + 1):
        at = slice(q * wide, (q + 1) * wide)
        part_ref[:, at] = lax.dot_general(
            ggu_ref[...], wgu_ref[at, :2 * hid], NT, preferred_element_type=F32
        ).astype(BF)
    size = 2 * block * ROWS
    out_row = iota((size, 1), 0)
    which, source, p = out_row // (block * ROWS), out_row // ROWS % block, out_row % ROWS
    slot_row = which * count + (p % CHUNKS) * few + p // CHUNKS * block + source
    tail_row = 2 * count + which * few + (p - cap) * block + source
    width = 2 * (count + few)
    perm = jnp.where(jnp.where(p < cap, slot_row, tail_row) == iota((size, width), 1), 1.0, 0.0).astype(BF)
    for b in range(blocks // 2):
        first = 2 * b * count
        at = slice(first, first + 2 * count)
        out = slice(b * size, (b + 1) * size)
        for q in range(CHUNKS):
            cols = slice(q * wide, (q + 1) * wide)
            pieces = [part_ref[at, cols]]
            for start in (first + q * few, first + count + q * few):
                pieces.append(part_ref[start:start + few, tail:])
            rhs = jnp.concatenate(pieces, axis=0)
            ret_ref[out, cols] = jnp.dot(perm, rhs, preferred_element_type=F32).astype(BF)
        ret_ref[out, tail:] = jnp.dot(perm[:, :2 * count], pair[at], preferred_element_type=F32).astype(BF)
        rows = pl.ds(b * size, size)
        stores.append(pltpu.make_async_copy(ret_ref.at[rows, :], ret_hbm.at[rows, :], out_sems.at[b]))
        stores[-1].start()
    for q in range(CHUNKS + 1):
        cols = pl.ds(q * wide, wide)
        at = slice(q * wide, (q + 1) * wide)
        down_ref[:, at] = lax.dot_general(hidden, scaled_ref[:, at], TN, preferred_element_type=F32).astype(BF)
        stores.append(pltpu.make_async_copy(down_ref.at[:, cols], down_hbm.at[:, cols], down_sems.at[q]))
        stores[-1].start()
    for store in stores:
        store.wait()


def unpack_down(packed_ref, down_ref):
    hid, dim = down_ref.shape
    lanes = packed_ref.shape[1] - hid
    high = 16 * (dim // 128)
    each = hid * high // packed_ref.shape[0]
    for part in range(packed_ref.shape[0] // high):
        for r in range(each // 16):
            for l in range(dim // 128):
                down_ref[part * each + r * 16:part * each + (r + 1) * 16, l * 128:(l + 1) * 128] = packed_ref[
                    part * high + l * 16:part * high + (l + 1) * 16, lanes + r * 128:lanes + (r + 1) * 128
                ]


def combine_kernel(gates_ref, back_ref, hot_ref, token_grad_ref, gate_grad_ref):
    toks, dim = token_grad_ref.shape
    wide = dim // (CHUNKS + 1)
    tail = CHUNKS * wide
    tails = None
    for q in range(CHUNKS):
        cols = slice(q * wide, (q + 1) * wide)
        moved = jnp.dot(hot_ref[q * 2 * toks:(q + 1) * 2 * toks, :], back_ref[:, cols], preferred_element_type=F32)
        token_grad_ref[:, cols] = moved[:toks].astype(BF)
        tails = moved[toks:] if tails is None else tails + moved[toks:]
    token_grad_ref[:, tail:] = tails.astype(BF)
    dots = jnp.dot(hot_ref[CHUNKS * 2 * toks:, :], back_ref[:, tail:], preferred_element_type=F32)
    gates = gates_ref[...].astype(F32)
    rows = []
    for k in range(2):
        pair = dots[k * toks:(k + 1) * toks].T
        rows.append((pair[0:1] + pair[1:2]) / gates[k:k + 1])
    gate_grad_ref[...] = jnp.concatenate(rows, axis=0).astype(BF)


def hot_kernel(experts, cap, routes_ref, after_ref, hot_ref):
    toks = routes_ref.shape[1]
    packed = experts * ROWS
    keys, first, _ = slot_keys(routes_ref, experts)
    spread = jnp.where(iota((experts, packed), 0) == iota((experts, packed), 1) // ROWS, 1.0, 0.0).astype(BF)
    key = lax.dot_general(keys.astype(BF), spread, TN, preferred_element_type=F32)
    one = lax.dot_general(jnp.where(first, 1.0, 0.0).astype(BF), spread, TN, preferred_element_type=F32)
    p = iota((1, packed), 1) % ROWS
    main_slot = jnp.where(p < cap, p, -2).astype(F32)
    main = jnp.where(key == main_slot, 1.0, 0.0)
    hot_ref[CHUNKS * 2 * toks:, :] = jnp.concatenate([main * one, main * (1.0 - one)], axis=0).astype(BF)
    for q in range(CHUNKS):
        slot = jnp.where(p < cap, -2, tail_slot(p, q, cap)).astype(F32)
        hot_ref[q * 2 * toks:(q + 1) * 2 * toks, :] = (
            jnp.concatenate([main, jnp.where(key == slot, 1.0, 0.0)], axis=0).astype(BF)
        )


VMEM = pl.BlockSpec(memory_space=pltpu.VMEM)
SMEM = pl.BlockSpec(memory_space=pltpu.SMEM)
HBM = pl.BlockSpec(memory_space=pltpu.HBM)


def call(kernel, ins, outs, scratch=(), limit=16, flops=0, moved=0):
    return pl.pallas_call(
        kernel,
        out_shape=tuple(jax.ShapeDtypeStruct(shape, kind) for shape, kind, _ in outs),
        in_specs=list(ins),
        out_specs=tuple(spec for _, _, spec in outs),
        scratch_shapes=list(scratch),
        compiler_params=pltpu.CompilerParams(vmem_limit_bytes=limit * 1024 * 1024),
        cost_estimate=pl.CostEstimate(flops=flops, bytes_accessed=moved, transcendentals=0),
    )


def local(tokens, routes, route_gates, out_grad, w_gate, w_up, w_down):
    experts = w_gate.shape[0] * lax.axis_size("expert")
    toks, fan_out = routes.shape
    dim = tokens.shape[1]
    hid = w_gate.shape[2]
    cap = 3 * toks * fan_out // (2 * experts)
    slots = experts * cap
    main = CHUNKS * dim // (CHUNKS + 1)
    packed = experts * ROWS
    DMA = pltpu.SemaphoreType.DMA
    routes_t = routes.T
    gates_t = route_gates.T
    share = dim // lax.axis_size("dp")
    send, mine = call(
        functools.partial(dispatch_kernel, experts, cap),
        (VMEM, VMEM, HBM, HBM, HBM, HBM, HBM),
        [((2 * packed, main), BF, HBM), ((share, 3 * hid), BF, HBM)],
        [
            pltpu.VMEM((toks, dim), BF), pltpu.VMEM((toks, dim), BF), pltpu.VMEM((2 * packed, main), BF),
            pltpu.VMEM(w_down.shape[1:], BF), pltpu.VMEM((share, 3 * hid), BF),
            DMA((2,)), DMA((experts // 16,)), DMA((4,)),
        ],
        limit=63, flops=8 * packed * toks * main, moved=4 * packed * main,
    )(routes_t, gates_t, tokens, out_grad, w_gate[0], w_up[0], w_down[0])
    weights = lax.all_gather(mine, "dp", axis=0, tiled=True)
    recv = lax.all_to_all(
        send.reshape(experts, 2 * ROWS, main), "expert", split_axis=0, concat_axis=0, tiled=True
    ).reshape(2 * packed, main)

    ret, down = call(
        functools.partial(expert_kernel, cap),
        (HBM, HBM),
        [((packed, main + 128), BF, HBM), ((hid, dim), BF, HBM)],
        [
            pltpu.VMEM((2 * packed, main), BF), pltpu.VMEM((dim, 3 * hid), BF), pltpu.VMEM((hid, dim), BF),
            pltpu.VMEM((slots, dim), BF), pltpu.VMEM((slots, dim), BF), pltpu.VMEM((slots, 2 * hid), BF),
            pltpu.VMEM((slots, dim), BF), pltpu.VMEM((packed, main + 128), BF), pltpu.VMEM((hid, dim), BF),
            DMA((2,)), DMA((experts // 16,)), DMA((experts // 32,)), DMA((CHUNKS + 1,)),
        ],
        limit=62, flops=12 * slots * dim * hid, moved=16 * slots * dim,
    )(recv, weights)
    down_grad = lax.psum_scatter(down, "dp", scatter_dimension=0, tiled=True)[None]
    back = lax.all_to_all(
        ret.reshape(experts, ROWS, main + 128), "expert", split_axis=0, concat_axis=0, tiled=True
    ).reshape(packed, main + 128)
    (hot,) = call(
        functools.partial(hot_kernel, experts, cap), (VMEM, HBM),
        [((2 * (CHUNKS + 1) * toks, packed), BF, VMEM)], flops=10**11, moved=10**9,
    )(routes_t, down_grad[0])
    token_grad, gate_grad = call(
        combine_kernel, (VMEM, VMEM, VMEM),
        [((toks, dim), BF, VMEM), ((fan_out, toks), BF, VMEM)],
        limit=16, flops=4 * toks * packed * dim, moved=4 * packed * dim,
    )(gates_t, back, hot)
    return token_grad, gate_grad.T, down_grad


def solution(mesh):
    rows = P(("dp", "expert"), None)
    weights = P("expert", "dp", None)
    return jax.shard_map(
        local,
        mesh=mesh,
        in_specs=(rows, rows, rows, rows, weights, weights, weights),
        out_specs=(rows, rows, weights),
        check_vma=False,
    )
```
